32 devices in a mesh: dp: 4 (over y, core), tensor: 8 (over z, x).
Axes of the slice: x: 2, y: 2, z: 4, core: 2. Of those that a mesh axis runs over, the one named last changes fastest.
Arguments:
- layer_input: bfloat16 [4096, 8192], P('dp', 'tensor'), may hold values from -6 to 6
- output_grad: bfloat16 [4096, 1024], P(('dp', 'tensor')), may hold values from -6 to 6
- key_weight: bfloat16 [8192, 1024], P('tensor'), may hold values from -0.0625 to 0.0625
- adapter_down: bfloat16 [128, 16, 8192], P('dp', None, 'tensor'), may hold values from -0.0625 to 0.0625
- adapter_up: bfloat16 [128, 16, 1024], P('dp', None, 'tensor'), may hold values from -0.1875 to 0.1875
- segment_adapter: int32 [32], replicated, may hold values from 0 to 127
- adapter_slot: int32 [128], replicated, may hold values from 0 to 127, each once
- live_segments: int32 [4], P('dp'), may hold values from 1 to 8, as said below
Outputs:
- input_grad: bfloat16 [4096, 8192], P('dp', 'tensor')
- down_grad: bfloat16 [128, 16, 8192], P('dp', None, 'tensor')
- up_grad: bfloat16 [128, 16, 1024], P('dp', None, 'tensor')
The draws below stay inside these ranges and needn't reach their ends.
Inputs may be any that keep to these rules, and one draw needn't show every extreme that they name: `live_segments`: some data group has all 8 segments live; a group's segments at or past its count are padding.
All inputs are finite; a program needn't handle non-finite values.
Results may differ from the reference program's by a relative error of at most 0.0057.
Values may be sent and summed in bfloat16 or wider, within the bound.
A program may use at most 64 MiB of HBM per device.

```python
import math
import jax
import jax.numpy as jnp
import numpy as np
from jax import lax

D = 8192
KW = 1024
R = 16
ADAPTERS = 128
SEG = 128
TOK_GROUP = 1024
TOKENS = 4096
SEGS_GROUP = 8
SEGS = 32
N_DP = 4


def draw_live_segments(key, part):
    base = jax.random.fold_in(key, 11)
    first_key, second_key = jax.random.split(base)
    counts = jax.random.randint(first_key, (N_DP,), 1, SEGS_GROUP + 1)
    full_group = jax.random.randint(second_key, (), 0, N_DP)
    filled = jnp.where(jnp.arange(N_DP) == full_group, SEGS_GROUP, counts)
    return filled.astype(jnp.int32)


def place_ends(values, own_key, low, largest):
    dims = values.shape
    spot = [jax.random.randint(jax.random.fold_in(own_key, axis), (), 0, dims[axis]) for axis in range(len(dims))]
    values = values.at[tuple(spot)].set(low)
    longest = dims.index(max(dims))
    spot[longest] = (spot[longest] + 1) % dims[longest]
    return values.at[tuple(spot)].set(largest)


def block_scale(own_key, extent, pieces, least, top_value):
    level = 1.0
    for position, parts in pieces:
        draws = jax.random.uniform(jax.random.fold_in(jax.random.fold_in(own_key, 6), position), (parts,), jnp.float32, least / len(pieces), top_value / len(pieces))
        level = level * jnp.repeat(jnp.exp(draws), extent[position] // parts).reshape((-1,) + (1,) * (len(extent) - 1 - position))
    return level


def rank_table(count, lean):
    weights = [(1 << 20) // math.isqrt(standing ** lean) + 1 for standing in range(1, count + 1)]
    width = 1 + sum(weights) // (1 << 30)
    return np.cumsum(np.array([max(1, weight // width) for weight in weights]))


def skewed_ids(key, shape, number_of, slope):
    table = rank_table(number_of, slope)
    pick = jax.random.randint(jax.random.fold_in(key, 1), shape, 0, int(table[number_of - 1]))
    grade = jnp.searchsorted(jnp.asarray(table, jnp.int32), pick, side="right")
    return jax.random.permutation(jax.random.fold_in(key, 2), number_of)[grade].astype(jnp.int32)


def noise(stream_key, extent, scale, limit, cuts=(), kind=jnp.bfloat16):
    values = scale * jax.random.normal(stream_key, extent, jnp.float32)
    if cuts:
        values = values * block_scale(stream_key, extent, cuts, -0.22, 0.18)
    return jnp.clip(values, -limit, limit).astype(kind)


def setup_inputs(seed: int = 0) -> dict:
    streams_of = jax.random.split(jax.random.key(seed), 9)
    return {
        "layer_input": noise(streams_of[0], (TOKENS, D), 1.0, 6.0, ((0, 4), (1, 8))),
        "output_grad": noise(streams_of[1], (TOKENS, KW), 1.0, 6.0, ((0, 32),)),
        "key_weight": noise(streams_of[2], (D, KW), D ** -0.5, 0.0625, ((0, 8),)),
        "adapter_down": noise(streams_of[3], (ADAPTERS, R, D), D ** -0.5, 0.0625, ((0, 4), (2, 8))),
        "adapter_up": noise(streams_of[4], (ADAPTERS, R, KW), KW ** -0.5, 0.1875, ((0, 4), (2, 8))),
        "segment_adapter": place_ends(skewed_ids(streams_of[5], (SEGS,), ADAPTERS, 2), jax.random.fold_in(streams_of[5], 3), 0, ADAPTERS - 1).astype(jnp.int32),
        "adapter_slot": jax.random.permutation(streams_of[6], ADAPTERS).astype(jnp.int32),
        "live_segments": draw_live_segments(jax.random.fold_in(streams_of[8], 71), 0),
    }


def reference(layer_input, output_grad, key_weight, adapter_down, adapter_up, segment_adapter, adapter_slot, live_segments):
    seg_slot = jnp.take(adapter_slot, segment_adapter, axis=0).astype(jnp.int32)
    positions = jnp.arange(SEGS_GROUP, dtype=jnp.int32)
    slot_ids = jnp.arange(ADAPTERS, dtype=jnp.int32)

    def one_group(totals, inputs):
        input_rows, grad_rows, slots, count = inputs
        live = (positions < count).astype(grad_rows.dtype)
        masked = grad_rows.reshape(SEGS_GROUP, SEG, KW) * live[:, None, None]
        down_seg = jnp.take(adapter_down, slots, axis=0).astype(jnp.float32)
        up_seg = jnp.take(adapter_up, slots, axis=0).astype(jnp.float32)
        masked_wide = masked.astype(jnp.float32)
        input_wide = input_rows.reshape(SEGS_GROUP, SEG, D).astype(jnp.float32)
        lowrank = jnp.einsum("sjk,srk->sjr", masked_wide, up_seg).astype(jnp.bfloat16)
        projected = jnp.einsum("sjd,srd->sjr", input_wide, down_seg).astype(jnp.bfloat16)
        frozen = jnp.dot(masked.reshape(TOK_GROUP, KW), key_weight.T, preferred_element_type=jnp.float32)
        extra = 2.0 * jnp.einsum("sjr,srd->sjd", lowrank.astype(jnp.float32), down_seg)
        input_grad = (frozen + extra.reshape(TOK_GROUP, D)).astype(jnp.bfloat16)
        seg_down = 2.0 * jnp.einsum("sjr,sjd->srd", lowrank.astype(jnp.float32), input_wide)
        seg_up = 2.0 * jnp.einsum("sjr,sjk->srk", projected.astype(jnp.float32), masked_wide)
        onehot = (slots[:, None] == slot_ids[None, :]).astype(jnp.float32)
        part_down = jnp.einsum("sa,srd->ard", onehot, seg_down, precision=lax.Precision.HIGHEST).astype(jnp.bfloat16)
        part_up = jnp.einsum("sa,srk->ark", onehot, seg_up, precision=lax.Precision.HIGHEST).astype(jnp.bfloat16)
        totals = (totals[0] + part_down.astype(jnp.float32), totals[1] + part_up.astype(jnp.float32))
        return totals, input_grad

    inputs = (layer_input.reshape(N_DP, TOK_GROUP, D), output_grad.reshape(N_DP, TOK_GROUP, KW), seg_slot.reshape(N_DP, SEGS_GROUP), live_segments)
    start = (jnp.zeros((ADAPTERS, R, D), jnp.float32), jnp.zeros((ADAPTERS, R, KW), jnp.float32))
    totals, input_grad = lax.scan(one_group, start, inputs)
    return input_grad.reshape(TOKENS, D), totals[0].astype(jnp.bfloat16), totals[1].astype(jnp.bfloat16)
```

```python
import functools

import jax
import jax.numpy as jnp
from jax import lax
from jax.experimental import pallas as pl
from jax.experimental.pallas import tpu as pltpu
from jax.sharding import PartitionSpec as P

MESH = pl.DeviceIdType.MESH
CHUNKS = 2
NT = (((1,), (1,)), ((), ()))
TN = (((0,), (0,)), ((), ()))


def fused_kernel(
    dims,
    adapter_s, slot_s, live_s,
    x_hbm, og_hbm, kw_hbm, ad_hbm, au_hbm,
    ig_hbm, dg_hbm, ug_hbm,
    seg_slot,
    x_v, kw_v, ad_v, au_v, og_v, whole, ig_v, dg_v, ug_v,
    s1d_out, s1u_out, s1d_in, s1u_in, s2d_out, s2u_out, s2d_in, s2u_in,
    down_seg, up_seg, up_own, lr, pr_out, pr_in, su_out, su_in, rows_d, rows_u,
    load_sem, store_sem, blk_send, blk_recv, s1_send, s1_recv, s2_send, s2_recv,
    up_send, up_recv, lr_send, lr_recv, pr_send, pr_recv, su_send, su_recv,
    rwy_send, rwc_send, rw_recv,
):
    T, X, Q, S, L, R, W, K, KS, PO = dims
    Z, Y = T // X, Q // 2
    half = L // CHUNKS
    t, q = lax.axis_index("tensor"), lax.axis_index("dp")
    z, x = t // X, lax.rem(t, X)
    y, c = q // 2, lax.rem(q, 2)
    mate = q + 1 - 2 * c
    pending = []

    def send(src, dst, send_sem, recv_sem, to, when=None):
        copy = pltpu.make_async_remote_copy(
            src_ref=src, dst_ref=dst, send_sem=send_sem, recv_sem=recv_sem,
            device_id=to, device_id_type=MESH,
        )
        if when is None:
            copy.start()
        else:
            pl.when(when)(copy.start)
        pending.append((when, copy))

    def arrived(ref, sem, when=None):
        copy = pltpu.make_async_copy(ref, ref, sem)
        if when is None:
            copy.wait()
        else:
            pl.when(when)(copy.wait)

    loads = [
        pltpu.make_async_copy(og_hbm, og_v, load_sem.at[0]),
        pltpu.make_async_copy(ad_hbm, ad_v, load_sem.at[1]),
        pltpu.make_async_copy(au_hbm, au_v, load_sem.at[2]),
        pltpu.make_async_copy(x_hbm, x_v, load_sem.at[3]),
        pltpu.make_async_copy(kw_hbm, kw_v, load_sem.at[4]),
    ]
    for copy in loads:
        copy.start()

    tensor_peers = [lax.rem(t + j, T) for j in range(1, T)]
    far = [lax.rem(y + j, Y) for j in range(1, Y)]
    barrier = pltpu.get_barrier_semaphore()
    for peer in tensor_peers:
        pl.semaphore_signal(barrier, inc=1, device_id={"tensor": peer}, device_id_type=MESH)
    pl.semaphore_signal(barrier, inc=1, device_id={"dp": mate}, device_id_type=MESH)
    for other in far:
        pl.semaphore_signal(barrier, inc=1, device_id={"dp": other * 2 + c}, device_id_type=MESH)

    for s in range(Q * S):
        seg_slot[s] = slot_s[adapter_s[s]]

    loads[0].wait()
    live = t < live_s[0]
    own_rows = jnp.where(live, og_v[...], jnp.zeros((L, K), jnp.bfloat16))
    whole[t] = own_rows

    def owned(index):
        local = seg_slot[index] - q * PO
        inside = jnp.logical_and(local >= 0, local < PO)
        return inside, jnp.clip(local, 0, PO - 1)

    loads[1].wait()
    loads[2].wait()

    def choose(i, carry):
        group, s = i // S, lax.rem(i, S)
        inside, local = owned((group * 2 + 1 - c) * S + s)
        s1u_out[group, s] = jnp.where(inside, au_v[local], jnp.zeros((R, KS), jnp.bfloat16))
        s1d_out[group, s] = jnp.where(inside, ad_v[local], jnp.zeros((R, W), jnp.bfloat16))
        return carry

    lax.fori_loop(0, Y * S, choose, 0)

    pl.semaphore_wait(barrier, T - 1 + 1 + Y - 1)

    def rows_of(origin, part):
        return whole.at[origin, pl.ds(part * half, half)]

    def to_z(origin, part, up, when):
        step = 1 if up else -1
        edge = (z + 1 < Z) if up else (z > 0)
        when = edge if when is None else jnp.logical_and(when, edge)
        ref = rows_of(origin, part)
        send(ref, ref, blk_send.at[origin, part, 0 if up else 1], blk_recv.at[origin, part],
             {"tensor": t + step * X}, when)

    def to_x(origin, part, when):
        ref = rows_of(origin, part)
        for j in range(1, X):
            to = z * X + lax.rem(x + j, X)
            send(ref, ref, blk_send.at[origin, part, 1 + j], blk_recv.at[origin, part],
                 {"tensor": to}, when)

    send(s1u_out, s1u_in, s1_send.at[1], s1_recv.at[1], {"dp": mate})
    send(s1d_out, s1d_in, s1_send.at[0], s1_recv.at[0], {"dp": mate})
    for part in range(CHUNKS):
        to_z(t, part, True, None)
        to_z(t, part, False, None)
        to_x(t, part, None)

    def forward(step, part):
        below, above = t - step * X, t + step * X
        has_below, has_above = z - step >= 0, z + step < Z
        below = jnp.where(has_below, below, 0)
        above = jnp.where(has_above, above, 0)
        arrived(rows_of(below, part), blk_recv.at[below, part], has_below)
        to_z(below, part, True, has_below)
        to_x(below, part, has_below)
        arrived(rows_of(above, part), blk_recv.at[above, part], has_above)
        to_z(above, part, False, has_above)
        to_x(above, part, has_above)

    def combine_up(i, carry):
        group, s = i // S, lax.rem(i, S)
        inside, local = owned((group * 2 + c) * S + s)
        s2u_out[group, s] = jnp.where(inside, au_v[local], s1u_in[group, s])
        return carry

    def combine_down(i, carry):
        group, s = i // S, lax.rem(i, S)
        inside, local = owned((group * 2 + c) * S + s)
        s2d_out[group, s] = jnp.where(inside, ad_v[local], s1d_in[group, s])
        return carry

    arrived(s1u_in, s1_recv.at[1])
    lax.fori_loop(0, Y * S, combine_up, 0)
    for other in far:
        send(s2u_out.at[other], s2u_in.at[y], s2_send.at[other, 1], s2_recv.at[y, 1],
             {"dp": other * 2 + c})
    arrived(s1d_in, s1_recv.at[0])
    lax.fori_loop(0, Y * S, combine_down, 0)
    for other in far:
        send(s2d_out.at[other], s2d_in.at[y], s2_send.at[other, 0], s2_recv.at[y, 0],
             {"dp": other * 2 + c})

    for other in far:
        arrived(s2u_in.at[other], s2_recv.at[other, 1])
    total = s2u_out[y]
    for other in far:
        total = total + s2u_in[other]
    up_seg[...] = total
    for peer in tensor_peers:
        send(up_seg.at[peer], up_own.at[t], up_send.at[peer], up_recv.at[t], {"tensor": peer})
    up_own[t] = up_seg[t]

    forward(1, 0)

    for peer in tensor_peers:
        arrived(up_own.at[peer], up_recv.at[peer])
    acc = jnp.zeros((R, L), jnp.float32)
    for p in range(T):
        acc = acc + lax.dot_general(
            up_own[p], whole[t, :, p * KS:(p + 1) * KS], NT, preferred_element_type=jnp.float32
        )
    lr[t] = acc.astype(jnp.bfloat16)
    for peer in tensor_peers:
        send(lr.at[t], lr.at[t], lr_send.at[peer], lr_recv.at[t], {"tensor": peer})

    forward(1, 1)

    for other in far:
        arrived(s2d_in.at[other], s2_recv.at[other, 0])
    loads[3].wait()

    def down_of(s, carry):
        rows = s2d_out[y, s]
        for other in far:
            rows = rows + s2d_in[other, s]
        down_seg[s] = rows
        pr_out[s] = lax.dot_general(rows, x_v[s], NT, preferred_element_type=jnp.float32)
        return carry

    lax.fori_loop(0, S, down_of, 0)
    for peer in tensor_peers:
        send(pr_out.at[peer], pr_in.at[t], pr_send.at[peer], pr_recv.at[t], {"tensor": peer})
    pr_in[t] = pr_out[t]

    for peer in tensor_peers:
        arrived(lr.at[peer], lr_recv.at[peer])

    own_slots = [seg_slot[q * S + s] for s in range(S)]

    def merged(parts, u, zero):
        return [jnp.where(own_slots[u] == own_slots[s], parts[s], zero) for s in range(S)]

    zero_l = jnp.zeros((R, L), jnp.bfloat16)
    ranks = [lr[s] for s in range(S)]
    left = jnp.concatenate(
        [jnp.concatenate(merged(ranks, u, zero_l), axis=1) for u in range(S)], axis=0
    )
    tile = 256
    for n in range(W // tile):
        columns = slice(n * tile, (n + 1) * tile)
        right = jnp.concatenate([x_v[s, :, columns] for s in range(S)], axis=0)
        grad = 2.0 * jnp.dot(left, right, preferred_element_type=jnp.float32)
        rows_d[q, :, :, columns] = grad.astype(jnp.bfloat16).reshape(S, R, tile)
    for other in far:
        send(rows_d.at[q], rows_d.at[q], rwy_send.at[other, 0], rw_recv.at[q, 0],
             {"dp": other * 2 + c})
    send(rows_d.at[q], rows_d.at[q], rwc_send.at[q, 0], rw_recv.at[q, 0], {"dp": mate})

    if Z > 2:
        forward(2, 0)

    for peer in tensor_peers:
        arrived(pr_in.at[peer], pr_recv.at[peer])
    acc = pr_in[0]
    for p in range(1, T):
        acc = acc + pr_in[p]
    projected = acc.astype(jnp.bfloat16)
    for p in range(T):
        su_out[p] = 2.0 * jnp.dot(
            projected, whole[t, :, p * KS:(p + 1) * KS], preferred_element_type=jnp.float32
        )
    for peer in tensor_peers:
        send(su_out.at[peer], su_in.at[t], su_send.at[peer], su_recv.at[t], {"tensor": peer})
    su_in[t] = su_out[t]

    if Z > 2:
        forward(2, 1)

    loads[4].wait()

    def block(origin):
        rank = lr[origin]

        def columns_of(n, carry):
            at = pl.ds(pl.multiple_of(n * tile, tile), tile)
            value = lax.dot_general(whole[origin], kw_v[at, :], NT, preferred_element_type=jnp.float32)
            extra = lax.dot_general(rank, down_seg[origin, :, at], TN, preferred_element_type=jnp.float32)
            ig_v[origin, :, at] = (value + 2.0 * extra).astype(jnp.bfloat16)
            return carry

        lax.fori_loop(0, W // tile, columns_of, 0)
        pltpu.make_async_copy(ig_v.at[origin], ig_hbm.at[origin], store_sem.at[origin]).start()

    def side_blocks(step):
        signs = (0,) if step == 0 else (-1, 1)
        for sign in signs:
            row = z + sign * step
            inside = jnp.logical_and(row >= 0, row < Z)
            for j in range(1, X):
                origin = jnp.where(inside, row, 0) * X + lax.rem(x + j, X)

                @pl.when(inside)
                def _():
                    for part in range(CHUNKS):
                        arrived(rows_of(origin, part), blk_recv.at[origin, part])
                    block(origin)

    def line_blocks(step):
        for sign in (-1, 1):
            row = z + sign * step
            inside = jnp.logical_and(row >= 0, row < Z)
            origin = jnp.where(inside, row, 0) * X + x

            @pl.when(inside)
            def _():
                block(origin)

    block(t)
    side_blocks(0)

    for peer in tensor_peers:
        arrived(su_in.at[peer], su_recv.at[peer])
    zero_u = jnp.zeros((R, KS), jnp.float32)
    for u in range(S):
        total = zero_u
        for s in range(S):
            total = total + jnp.where(own_slots[u] == own_slots[s], su_in[s], zero_u)
        rows_u[q, u] = total.astype(jnp.bfloat16)
    for other in far:
        send(rows_u.at[q], rows_u.at[q], rwy_send.at[other, 1], rw_recv.at[q, 1],
             {"dp": other * 2 + c})
    send(rows_u.at[q], rows_u.at[q], rwc_send.at[q, 1], rw_recv.at[q, 1], {"dp": mate})

    line_blocks(1)
    for step in range(3, Z):
        forward(step, 0)

    for kind, rows in ((0, rows_d), (1, rows_u)):
        for other in far:
            origin = other * 2 + c
            arrived(rows.at[origin], rw_recv.at[origin, kind])
            send(rows.at[origin], rows.at[origin], rwc_send.at[origin, kind],
                 rw_recv.at[origin, kind], {"dp": mate})

    side_blocks(1)
    for step in range(3, Z):
        forward(step, 1)
    for step in range(2, Z):
        line_blocks(step)

    for kind, rows in ((0, rows_d), (1, rows_u)):
        for group in range(Y):
            origin = group * 2 + 1 - c
            arrived(rows.at[origin], rw_recv.at[origin, kind])

    def owner_rows(p, carry):
        down_total = jnp.zeros((R, W), jnp.float32)
        up_total = jnp.zeros((R, KS), jnp.float32)
        slot = q * PO + p
        for group in range(Q):
            index = jnp.int32(0)
            found = jnp.int32(0)
            for s in reversed(range(S)):
                match = seg_slot[group * S + s] == slot
                index = jnp.where(match, jnp.int32(s), index)
                found = jnp.where(match, jnp.int32(1), found)
            has = found == 1
            down_total += jnp.where(has, rows_d[group, index].astype(jnp.float32), 0.0)
            up_total += jnp.where(has, rows_u[group, index].astype(jnp.float32), 0.0)
        dg_v[p] = down_total.astype(jnp.bfloat16)
        ug_v[p] = up_total.astype(jnp.bfloat16)
        return carry

    lax.fori_loop(0, PO, owner_rows, 0)
    stores = [
        pltpu.make_async_copy(dg_v, dg_hbm, store_sem.at[T]),
        pltpu.make_async_copy(ug_v, ug_hbm, store_sem.at[T + 1]),
    ]
    for copy in stores:
        copy.start()

    for step in range(2, Z):
        side_blocks(step)

    for when, copy in pending:
        if when is None:
            copy.wait_send()
        else:
            pl.when(when)(copy.wait_send)
    for origin in range(T):
        pltpu.make_async_copy(ig_v.at[origin], ig_hbm.at[origin], store_sem.at[origin]).wait()
    for copy in stores:
        copy.wait()


def fused(layer_input, output_grad, key_weight, adapter_down, adapter_up, segment_adapter, adapter_slot, live_segments):
    T, Q = lax.axis_size("tensor"), lax.axis_size("dp")
    X = 1 << ((T.bit_length() - 1) // 2)
    W = layer_input.shape[1]
    L, K = output_grad.shape
    PO, R, KS = adapter_up.shape
    S = segment_adapter.shape[0] // Q
    Y = Q // 2
    dims = (T, X, Q, S, L, R, W, K, KS, PO)
    bf, f32 = jnp.bfloat16, jnp.float32
    V, DMA = pltpu.VMEM, pltpu.SemaphoreType.DMA
    smem = pl.BlockSpec(memory_space=pltpu.SMEM)
    hbm = pl.BlockSpec(memory_space=pl.ANY)
    flops = 2 * T * L * K * W + 8 * T * L * R * W
    input_grad, down_grad, up_grad = pl.pallas_call(
        functools.partial(fused_kernel, dims),
        out_shape=(
            jax.ShapeDtypeStruct((T, L, W), bf),
            jax.ShapeDtypeStruct((PO, R, W), bf),
            jax.ShapeDtypeStruct((PO, R, KS), bf),
        ),
        in_specs=[smem] * 3 + [hbm] * 5,
        out_specs=(hbm,) * 3,
        scratch_shapes=[
            pltpu.SMEM((Q * S,), jnp.int32),
            V((T, L, W), bf), V((W, K), bf), V((PO, R, W), bf), V((PO, R, KS), bf), V((L, K), bf),
            V((T, L, K), bf), V((T, L, W), bf), V((PO, R, W), bf), V((PO, R, KS), bf),
            V((Y, S, R, W), bf), V((Y, S, R, KS), bf), V((Y, S, R, W), bf), V((Y, S, R, KS), bf),
            V((Y, S, R, W), bf), V((Y, S, R, KS), bf), V((Y, S, R, W), bf), V((Y, S, R, KS), bf),
            V((S, R, W), bf), V((S, R, KS), bf), V((T, R, KS), bf), V((T, R, L), bf),
            V((S, R, L), f32), V((T, R, L), f32), V((T, R, KS), f32), V((T, R, KS), f32),
            V((Q, S, R, W), bf), V((Q, S, R, KS), bf),
            DMA((5,)), DMA((T + 2,)), DMA((T, CHUNKS, 1 + X)), DMA((T, CHUNKS)),
            DMA((2,)), DMA((2,)), DMA((Y, 2)), DMA((Y, 2)),
            DMA((T,)), DMA((T,)), DMA((T,)), DMA((T,)),
            DMA((T,)), DMA((T,)), DMA((T,)), DMA((T,)),
            DMA((Y, 2)), DMA((Q, 2)), DMA((Q, 2)),
        ],
        compiler_params=pltpu.CompilerParams(
            collective_id=0, has_side_effects=True, vmem_limit_bytes=48 * 1024 * 1024
        ),
        cost_estimate=pl.CostEstimate(
            flops=flops, bytes_accessed=2 * (2 * T * L * W + K * W + 2 * PO * R * W), transcendentals=0
        ),
    )(
        segment_adapter, adapter_slot, live_segments,
        layer_input.reshape(T, L, W), output_grad, key_weight, adapter_down, adapter_up,
    )
    return input_grad.reshape(T * L, W), down_grad, up_grad


def on_device(
    layer_input,
    output_grad,
    key_weight,
    adapter_down,
    adapter_up,
    segment_adapter,
    adapter_slot,
    live_segments,
):
    tensor_size = lax.axis_size("tensor")
    position = lax.axis_index("tensor")
    group_count = lax.axis_size("dp")
    group_index = lax.axis_index("dp")
    row_count = output_grad.shape[0]
    tok_group = layer_input.shape[0]
    width_shard = layer_input.shape[1]
    key_width = output_grad.shape[1]
    key_shard = key_width // tensor_size
    adapters = adapter_slot.shape[0]
    rank_dim = adapter_down.shape[1]
    seg_total = segment_adapter.shape[0]
    seg_group = seg_total // group_count
    seg_len = tok_group // seg_group
    per_owner = adapters // group_count
    slot_ids = jnp.arange(adapters, dtype=jnp.int32)
    lookup = segment_adapter[:, None] == slot_ids[None, :]
    every_slot = jnp.sum(jnp.where(lookup, adapter_slot[None, :], 0), axis=1)
    seg_slot = lax.dynamic_slice_in_dim(every_slot, group_index * seg_group, seg_group)
    local_rows = position * row_count + jnp.arange(row_count, dtype=jnp.int32)
    live_rows = local_rows // seg_len < live_segments[0]
    masked = jnp.where(live_rows[:, None], output_grad, jnp.zeros_like(output_grad))
    whole = lax.all_gather(masked, "tensor", axis=0, tiled=True)
    stores = (
        lax.all_gather(adapter_down, "dp", axis=0, tiled=True),
        lax.all_gather(adapter_up, "dp", axis=0, tiled=True),
    )
    choose = (seg_slot[:, None] == slot_ids[None, :]).astype(jnp.bfloat16)
    down_seg = jnp.dot(choose, stores[0].reshape(adapters, -1), preferred_element_type=jnp.float32)
    down_seg = down_seg.astype(jnp.bfloat16).reshape(seg_group, rank_dim, width_shard)
    up_seg = jnp.dot(choose, stores[1].reshape(adapters, -1), preferred_element_type=jnp.float32)
    up_seg = up_seg.astype(jnp.bfloat16).reshape(seg_group, rank_dim, key_shard)
    own_keys = lax.dynamic_slice_in_dim(whole, position * key_shard, key_shard, 1).reshape(
        seg_group, seg_len, key_shard
    )
    input_seg = layer_input.reshape(seg_group, seg_len, width_shard)
    up_part = jnp.einsum("sjk,srk->rsj", own_keys, up_seg, preferred_element_type=jnp.float32)
    down_part = jnp.einsum("sjd,srd->rsj", input_seg, down_seg, preferred_element_type=jnp.float32)
    lowrank, projected = lax.psum((up_part, down_part), "tensor")
    lowrank = lowrank.astype(jnp.bfloat16)
    projected = projected.astype(jnp.bfloat16)
    frozen = lax.dot_general(
        whole, key_weight, (((1,), (1,)), ((), ())), preferred_element_type=jnp.float32
    )
    extra = jnp.einsum("rsj,srd->sjd", lowrank, down_seg, preferred_element_type=jnp.float32)
    input_grad = (frozen + 2.0 * extra.reshape(tok_group, width_shard)).astype(jnp.bfloat16)
    seg_down = 2.0 * jnp.einsum(
        "rsj,sjd->srd", lowrank, input_seg, preferred_element_type=jnp.float32
    )
    seg_up = 2.0 * jnp.einsum(
        "rsj,sjk->srk", projected, own_keys, preferred_element_type=jnp.float32
    )
    seg_index = jnp.arange(seg_group, dtype=jnp.int32)
    same = seg_slot[:, None] == seg_slot[None, :]
    earlier = same & (seg_index[None, :] < seg_index[:, None])
    leading = jnp.logical_not(jnp.any(earlier, axis=1))
    merge_rows = (same & leading[:, None]).astype(jnp.float32)
    rows_down = jnp.einsum(
        "us,srd->urd", merge_rows, seg_down, precision=lax.Precision.HIGHEST
    ).astype(jnp.bfloat16)
    rows_up = jnp.einsum("us,srk->urk", merge_rows, seg_up, precision=lax.Precision.HIGHEST).astype(
        jnp.bfloat16
    )
    every_down, every_up = (
        lax.all_gather(rows_down, "dp", axis=0, tiled=True),
        lax.all_gather(rows_up, "dp", axis=0, tiled=True),
    )
    owned = group_index * per_owner + jnp.arange(per_owner, dtype=jnp.int32)
    mine = (every_slot[:, None] == owned[None, :]).astype(jnp.bfloat16)
    down_grad = jnp.einsum(
        "sp,srd->prd", mine, every_down, preferred_element_type=jnp.float32
    ).astype(jnp.bfloat16)
    up_grad = jnp.einsum("sp,srk->prk", mine, every_up, preferred_element_type=jnp.float32).astype(
        jnp.bfloat16
    )
    return (input_grad, down_grad, up_grad)


def device_program(layer_input, output_grad, key_weight, adapter_down, adapter_up, segment_adapter, adapter_slot, live_segments):
    args = (layer_input, output_grad, key_weight, adapter_down, adapter_up, segment_adapter, adapter_slot, live_segments)
    seg_group = segment_adapter.shape[0] // lax.axis_size("dp")
    one_each = seg_group == lax.axis_size("tensor")
    tiled = adapter_up.shape[2] % 128 == 0 and layer_input.shape[1] % 256 == 0
    if one_each and tiled and lax.axis_size("dp") % 2 == 0:
        return fused(*args)
    return on_device(*args)


def solution(mesh):
    in_specs = (
        P("dp", "tensor"),
        P(("dp", "tensor"), None),
        P("tensor", None),
        P("dp", None, "tensor"),
        P("dp", None, "tensor"),
        P(),
        P(),
        P("dp"),
    )
    out_specs = (P("dp", "tensor"), P("dp", None, "tensor"), P("dp", None, "tensor"))
    return jax.shard_map(
        device_program, mesh=mesh, in_specs=in_specs, out_specs=out_specs, check_vma=False
    )
```

```python
import functools

import jax
import jax.numpy as jnp
from jax import lax
from jax.experimental import pallas as pl
from jax.experimental.pallas import tpu as pltpu
from jax.sharding import PartitionSpec as P

MESH = pl.DeviceIdType.MESH
CHUNKS = 4
NT = (((1,), (1,)), ((), ()))
TN = (((0,), (0,)), ((), ()))


def fused_kernel(
    dims,
    adapter_hbm, slot_hbm, live_hbm,
    x_hbm, og_hbm, kw_hbm, ad_hbm, au_hbm,
    ig_hbm, dg_hbm, ug_hbm,
    adapter_s, slot_s, live_s, seg_slot,
    x_v, kw_v, ad_v, au_v, og_v, whole, ig_v, dg_v, ug_v,
    s1d_out, s1d_in, s2d_out, s2d_in, fu_out, fu_in,
    down_seg, up_seg, up_own, lr, pr_out, pr_in, su_out, su_in, rows_d, rows_u,
    load_sem, store_sem, blk_send, blk_recv, s1_send, s1_recv, s2_send, s2_recv, fu_send, fu_recv,
    up_send, up_recv, lr_send, lr_recv, pr_send, pr_recv, su_send, su_recv,
    rwy_send, rwu_send, rwc_send, rw_recv,
):
    T, X, Q, S, L, R, W, K, KS, PO = dims
    Z, Y = T // X, Q // 2
    half = L // CHUNKS
    t, q = lax.axis_index("tensor"), lax.axis_index("dp")
    z, x = t // X, lax.rem(t, X)
    y, c = q // 2, lax.rem(q, 2)
    mate = q + 1 - 2 * c
    pending = []

    def send(src, dst, send_sem, recv_sem, to, when=None):
        copy = pltpu.make_async_remote_copy(
            src_ref=src, dst_ref=dst, send_sem=send_sem, recv_sem=recv_sem,
            device_id=to, device_id_type=MESH,
        )
        if when is None:
            copy.start()
        else:
            pl.when(when)(copy.start)
        pending.append((when, copy))

    def arrived(ref, sem, when=None):
        copy = pltpu.make_async_copy(ref, ref, sem)
        if when is None:
            copy.wait()
        else:
            pl.when(when)(copy.wait)

    scalars = [
        pltpu.make_async_copy(adapter_hbm, adapter_s, load_sem.at[5]),
        pltpu.make_async_copy(slot_hbm, slot_s, load_sem.at[6]),
        pltpu.make_async_copy(live_hbm, live_s, load_sem.at[7]),
    ]
    loads = [
        pltpu.make_async_copy(og_hbm, og_v, load_sem.at[0]),
        pltpu.make_async_copy(au_hbm, au_v, load_sem.at[2]),
        pltpu.make_async_copy(ad_hbm, ad_v, load_sem.at[1]),
    ]
    later_loads = [
        pltpu.make_async_copy(x_hbm, x_v, load_sem.at[3]),
        pltpu.make_async_copy(kw_hbm, kw_v, load_sem.at[4]),
    ]
    for copy in scalars + loads:
        copy.start()

    tensor_peers = [lax.rem(t + j, T) for j in range(1, T)]
    far = [lax.rem(y + j, Y) for j in range(1, Y)]
    barrier = pltpu.get_barrier_semaphore()
    for peer in tensor_peers:
        pl.semaphore_signal(barrier, inc=1, device_id={"tensor": peer}, device_id_type=MESH)
    dp_peers = [lax.rem(q + j, Q) for j in range(1, Q)]
    for peer in dp_peers:
        pl.semaphore_signal(barrier, inc=1, device_id={"dp": peer}, device_id_type=MESH)

    for copy in scalars:
        copy.wait()
    for s in range(Q * S):
        seg_slot[s] = slot_s[adapter_s[s]]

    loads[0].wait()
    live = t < live_s[0]
    own_rows = jnp.where(live, og_v[...], jnp.zeros((L, K), jnp.bfloat16))
    whole[t] = own_rows

    def owned(index):
        local = seg_slot[index] - q * PO
        inside = jnp.logical_and(local >= 0, local < PO)
        return inside, jnp.clip(local, 0, PO - 1)

    loads[1].wait()

    def choose_up(i, carry):
        group, s = i // S, lax.rem(i, S)
        inside, local = owned(i)
        fu_out[group, s] = jnp.where(inside, au_v[local], jnp.zeros((R, KS), jnp.bfloat16))
        return carry

    lax.fori_loop(0, Q * S, choose_up, 0)

    loads[2].wait()

    def choose_down(i, carry):
        group, s = i // S, lax.rem(i, S)
        inside, local = owned((group * 2 + 1 - c) * S + s)
        s1d_out[group, s] = jnp.where(inside, ad_v[local], jnp.zeros((R, W), jnp.bfloat16))
        return carry

    lax.fori_loop(0, Y * S, choose_down, 0)
    for copy in later_loads:
        copy.start()

    pl.semaphore_wait(barrier, T - 1 + Q - 1)

    def rows_of(origin, part):
        return whole.at[origin, pl.ds(part * half, half)]

    def to_z(origin, part, up, when):
        step = 1 if up else -1
        edge = (z + 1 < Z) if up else (z > 0)
        when = edge if when is None else jnp.logical_and(when, edge)
        ref = rows_of(origin, part)
        send(ref, ref, blk_send.at[origin, part, 0 if up else 1], blk_recv.at[origin, part],
             {"tensor": t + step * X}, when)

    def to_x(origin, part, when):
        ref = rows_of(origin, part)
        for j in range(1, X):
            to = z * X + lax.rem(x + j, X)
            send(ref, ref, blk_send.at[origin, part, 1 + j], blk_recv.at[origin, part],
                 {"tensor": to}, when)

    for peer in dp_peers:
        send(fu_out.at[peer], fu_in.at[q], fu_send.at[peer], fu_recv.at[q], {"dp": peer})
    send(s1d_out, s1d_in, s1_send.at[0], s1_recv.at[0], {"dp": mate})
    paired = X == 2 and Z % 2 == 0
    direct = CHUNKS // 2 if paired else CHUNKS
    pair_z = z + 1 - 2 * lax.rem(z, 2)
    column = z * X + lax.rem(x + 1, X)
    for part in range(CHUNKS):
        to_z(t, part, True, None)
        to_z(t, part, False, None)
        to_x(t, part, None)

    def forward(step, part):
        for sign in (-1, 1):
            row = z + sign * step
            inside = jnp.logical_and(row >= 0, row < Z)
            origin = jnp.where(inside, row, z) * X + x
            arrived(rows_of(origin, part), blk_recv.at[origin, part], inside)
            to_z(origin, part, sign < 0, inside)
            across = inside
            if part >= direct:
                across = jnp.logical_and(inside, row != pair_z)
            to_x(origin, part, across)

    def share(part):
        if paired:
            ref = rows_of(column, part)
            arrived(ref, blk_recv.at[column, part])
            send(ref, ref, blk_send.at[column, part, 0], blk_recv.at[column, part],
                 {"tensor": pair_z * X + x})

    def combine_down(i, carry):
        group, s = i // S, lax.rem(i, S)
        inside, local = owned((group * 2 + c) * S + s)
        s2d_out[group, s] = jnp.where(inside, ad_v[local], s1d_in[group, s])
        return carry

    arrived(s1d_in, s1_recv.at[0])
    lax.fori_loop(0, Y * S, combine_down, 0)
    for other in far:
        send(s2d_out.at[other], s2d_in.at[y], s2_send.at[other, 0], s2_recv.at[y, 0],
             {"dp": other * 2 + c})

    forward(1, 0)

    total = fu_out[q]
    for peer in dp_peers:
        arrived(fu_in.at[peer], fu_recv.at[peer])
        total = total + fu_in[peer]
    up_seg[...] = total
    for peer in tensor_peers:
        send(up_seg.at[peer], up_own.at[t], up_send.at[peer], up_recv.at[t], {"tensor": peer})
    up_own[t] = up_seg[t]

    forward(1, 1)
    forward(1, 2)

    for peer in tensor_peers:
        arrived(up_own.at[peer], up_recv.at[peer])
    acc = jnp.zeros((R, L), jnp.float32)
    for p in range(T):
        acc = acc + lax.dot_general(
            up_own[p], whole[t, :, p * KS:(p + 1) * KS], NT, preferred_element_type=jnp.float32
        )
    lr[t] = acc.astype(jnp.bfloat16)
    for peer in tensor_peers:
        send(lr.at[t], lr.at[t], lr_send.at[peer], lr_recv.at[t], {"tensor": peer})

    share(2)
    forward(1, 3)
    share(3)
    if Z > 2:
        forward(2, 0)

    for other in far:
        arrived(s2d_in.at[other], s2_recv.at[other, 0])
    later_loads[0].wait()

    def down_of(s, carry):
        rows = s2d_out[y, s]
        for other in far:
            rows = rows + s2d_in[other, s]
        down_seg[s] = rows
        pr_out[s] = lax.dot_general(rows, x_v[s], NT, preferred_element_type=jnp.float32)
        return carry

    lax.fori_loop(0, S, down_of, 0)
    for peer in tensor_peers:
        send(pr_out.at[peer], pr_in.at[t], pr_send.at[peer], pr_recv.at[t], {"tensor": peer})
    pr_in[t] = pr_out[t]

    if Z > 2:
        forward(2, 1)

    for peer in tensor_peers:
        arrived(lr.at[peer], lr_recv.at[peer])

    own_slots = [seg_slot[q * S + s] for s in range(S)]

    def merged(parts, u, zero):
        return [jnp.where(own_slots[u] == own_slots[s], parts[s], zero) for s in range(S)]

    zero_l = jnp.zeros((R, L), jnp.bfloat16)
    ranks = [lr[s] for s in range(S)]
    left = jnp.concatenate(
        [jnp.concatenate(merged(ranks, u, zero_l), axis=1) for u in range(S)], axis=0
    )
    tile = 256
    for n in range(W // tile):
        columns = slice(n * tile, (n + 1) * tile)
        right = jnp.concatenate([x_v[s, :, columns] for s in range(S)], axis=0)
        grad = 2.0 * jnp.dot(left, right, preferred_element_type=jnp.float32)
        rows_d[q, :, :, columns] = grad.astype(jnp.bfloat16).reshape(S, R, tile)
    for other in far:
        send(rows_d.at[q], rows_d.at[q], rwy_send.at[other], rw_recv.at[q, 0],
             {"dp": other * 2 + c})
    send(rows_d.at[q], rows_d.at[q], rwc_send.at[q], rw_recv.at[q, 0], {"dp": mate})

    if Z > 2:
        forward(2, 2)

    later_loads[1].wait()

    def block_row(row):
        left_rows = whole[pl.ds(row * X, X)].reshape(X * L, K)
        for n in range(W // tile):
            at = slice(n * tile, (n + 1) * tile)
            value = lax.dot_general(left_rows, kw_v[at, :], NT, preferred_element_type=jnp.float32)
            for j in range(X):
                origin = row * X + j
                extra = lax.dot_general(
                    lr[origin], down_seg[origin, :, at], TN, preferred_element_type=jnp.float32
                )
                ig_v[origin, :, at] = (value[j * L:(j + 1) * L] + 2.0 * extra).astype(jnp.bfloat16)
        rows = pl.ds(row * X, X)
        pltpu.make_async_copy(ig_v.at[rows], ig_hbm.at[rows], store_sem.at[row]).start()

    def wait_side(row, parts):
        for j in range(1, X):
            origin = row * X + lax.rem(x + j, X)
            for part in parts:
                arrived(rows_of(origin, part), blk_recv.at[origin, part])

    def nearest(i):
        low, high = z, Z - 1 - z
        both = jnp.minimum(low, high)
        near = z + (-1 if i % 2 else 1) * ((i + 1) // 2)
        beyond = jnp.where(low < high, z + (i - both), z - (i - both))
        return jnp.where(i <= 2 * both, near, beyond)

    wait_side(z, range(direct))
    block_row(z)
    if Z > 2:
        forward(2, 3)

    for peer in tensor_peers:
        arrived(pr_in.at[peer], pr_recv.at[peer])
    acc = pr_in[0]
    for p in range(1, T):
        acc = acc + pr_in[p]
    projected = acc.astype(jnp.bfloat16)
    for p in range(T):
        su_out[p] = 2.0 * jnp.dot(
            projected, whole[t, :, p * KS:(p + 1) * KS], preferred_element_type=jnp.float32
        )
    for peer in tensor_peers:
        send(su_out.at[peer], su_in.at[t], su_send.at[peer], su_recv.at[t], {"tensor": peer})
    su_in[t] = su_out[t]

    for step in range(3, Z):
        forward(step, 0)
    wait_side(nearest(1), range(CHUNKS))
    block_row(nearest(1))
    for step in range(3, Z):
        forward(step, 1)

    for peer in tensor_peers:
        arrived(su_in.at[peer], su_recv.at[peer])
    zero_u = jnp.zeros((R, KS), jnp.float32)
    for u in range(S):
        total = zero_u
        for s in range(S):
            total = total + jnp.where(own_slots[u] == own_slots[s], su_in[s], zero_u)
        rows_u[q, u] = total.astype(jnp.bfloat16)
    for peer in dp_peers:
        send(rows_u.at[q], rows_u.at[q], rwu_send.at[peer], rw_recv.at[q, 1], {"dp": peer})

    for step in range(3, Z):
        forward(step, 2)
    for other in far:
        origin = other * 2 + c
        arrived(rows_d.at[origin], rw_recv.at[origin, 0])
        send(rows_d.at[origin], rows_d.at[origin], rwc_send.at[origin],
             rw_recv.at[origin, 0], {"dp": mate})
    for step in range(3, Z):
        forward(step, 3)

    for i in range(2, Z - 1):
        wait_side(nearest(i), range(CHUNKS))
        block_row(nearest(i))

    for group in range(Y):
        origin = group * 2 + 1 - c
        arrived(rows_d.at[origin], rw_recv.at[origin, 0])
    for peer in dp_peers:
        arrived(rows_u.at[peer], rw_recv.at[peer, 1])

    def owner_rows(p, carry):
        down_total = jnp.zeros((R, W), jnp.float32)
        up_total = jnp.zeros((R, KS), jnp.float32)
        slot = q * PO + p
        for group in range(Q):
            index = jnp.int32(0)
            found = jnp.int32(0)
            for s in reversed(range(S)):
                match = seg_slot[group * S + s] == slot
                index = jnp.where(match, jnp.int32(s), index)
                found = jnp.where(match, jnp.int32(1), found)
            has = found == 1
            down_total += jnp.where(has, rows_d[group, index].astype(jnp.float32), 0.0)
            up_total += jnp.where(has, rows_u[group, index].astype(jnp.float32), 0.0)
        dg_v[p] = down_total.astype(jnp.bfloat16)
        ug_v[p] = up_total.astype(jnp.bfloat16)
        return carry

    lax.fori_loop(0, PO, owner_rows, 0)
    stores = [
        pltpu.make_async_copy(dg_v, dg_hbm, store_sem.at[Z]),
        pltpu.make_async_copy(ug_v, ug_hbm, store_sem.at[Z + 1]),
    ]
    for copy in stores:
        copy.start()

    if Z > 2:
        wait_side(nearest(Z - 1), range(CHUNKS))
        block_row(nearest(Z - 1))

    for when, copy in pending:
        if when is None:
            copy.wait_send()
        else:
            pl.when(when)(copy.wait_send)
    for row in range(Z):
        rows = pl.ds(row * X, X)
        pltpu.make_async_copy(ig_v.at[rows], ig_hbm.at[rows], store_sem.at[row]).wait()
    for copy in stores:
        copy.wait()


def fused(layer_input, output_grad, key_weight, adapter_down, adapter_up, segment_adapter, adapter_slot, live_segments):
    T, Q = lax.axis_size("tensor"), lax.axis_size("dp")
    X = 1 << ((T.bit_length() - 1) // 2)
    W = layer_input.shape[1]
    L, K = output_grad.shape
    PO, R, KS = adapter_up.shape
    S = segment_adapter.shape[0] // Q
    Y = Q // 2
    dims = (T, X, Q, S, L, R, W, K, KS, PO)
    bf, f32 = jnp.bfloat16, jnp.float32
    V, DMA = pltpu.VMEM, pltpu.SemaphoreType.DMA
    far_in = pl.BlockSpec(memory_space=pltpu.HBM)
    hbm = pl.BlockSpec(memory_space=pl.ANY)
    flops = 2 * T * L * K * W + 8 * T * L * R * W
    input_grad, down_grad, up_grad = pl.pallas_call(
        functools.partial(fused_kernel, dims),
        out_shape=(
            jax.ShapeDtypeStruct((T, L, W), bf),
            jax.ShapeDtypeStruct((PO, R, W), bf),
            jax.ShapeDtypeStruct((PO, R, KS), bf),
        ),
        in_specs=[far_in] * 8,
        out_specs=(hbm,) * 3,
        scratch_shapes=[
            pltpu.SMEM((Q * S,), jnp.int32), pltpu.SMEM((adapter_slot.shape[0],), jnp.int32),
            pltpu.SMEM((1,), jnp.int32), pltpu.SMEM((Q * S,), jnp.int32),
            V((T, L, W), bf), V((W, K), bf), V((PO, R, W), bf), V((PO, R, KS), bf), V((L, K), bf),
            V((T, L, K), bf), V((T, L, W), bf), V((PO, R, W), bf), V((PO, R, KS), bf),
            V((Y, S, R, W), bf), V((Y, S, R, W), bf), V((Y, S, R, W), bf), V((Y, S, R, W), bf),
            V((Q, S, R, KS), bf), V((Q, S, R, KS), bf),
            V((S, R, W), bf), V((S, R, KS), bf), V((T, R, KS), bf), V((T, R, L), bf),
            V((S, R, L), f32), V((T, R, L), f32), V((T, R, KS), f32), V((T, R, KS), f32),
            V((Q, S, R, W), bf), V((Q, S, R, KS), bf),
            DMA((8,)), DMA((T + 2,)), DMA((T, CHUNKS, 1 + X)), DMA((T, CHUNKS)),
            DMA((2,)), DMA((2,)), DMA((Y, 2)), DMA((Y, 2)), DMA((Q,)), DMA((Q,)),
            DMA((T,)), DMA((T,)), DMA((T,)), DMA((T,)),
            DMA((T,)), DMA((T,)), DMA((T,)), DMA((T,)),
            DMA((Y,)), DMA((Q,)), DMA((Q,)), DMA((Q, 2)),
        ],
        compiler_params=pltpu.CompilerParams(
            collective_id=0, has_side_effects=True, vmem_limit_bytes=48 * 1024 * 1024
        ),
        cost_estimate=pl.CostEstimate(
            flops=flops, bytes_accessed=2 * (2 * T * L * W + K * W + 2 * PO * R * W), transcendentals=0
        ),
    )(
        segment_adapter, adapter_slot, live_segments,
        layer_input.reshape(T, L, W), output_grad, key_weight, adapter_down, adapter_up,
    )
    return input_grad.reshape(T * L, W), down_grad, up_grad


def on_device(
    layer_input,
    output_grad,
    key_weight,
    adapter_down,
    adapter_up,
    segment_adapter,
    adapter_slot,
    live_segments,
):
    tensor_size = lax.axis_size("tensor")
    position = lax.axis_index("tensor")
    group_count = lax.axis_size("dp")
    group_index = lax.axis_index("dp")
    row_count = output_grad.shape[0]
    tok_group = layer_input.shape[0]
    width_shard = layer_input.shape[1]
    key_width = output_grad.shape[1]
    key_shard = key_width // tensor_size
    adapters = adapter_slot.shape[0]
    rank_dim = adapter_down.shape[1]
    seg_total = segment_adapter.shape[0]
    seg_group = seg_total // group_count
    seg_len = tok_group // seg_group
    per_owner = adapters // group_count
    slot_ids = jnp.arange(adapters, dtype=jnp.int32)
    lookup = segment_adapter[:, None] == slot_ids[None, :]
    every_slot = jnp.sum(jnp.where(lookup, adapter_slot[None, :], 0), axis=1)
    seg_slot = lax.dynamic_slice_in_dim(every_slot, group_index * seg_group, seg_group)
    local_rows = position * row_count + jnp.arange(row_count, dtype=jnp.int32)
    live_rows = local_rows // seg_len < live_segments[0]
    masked = jnp.where(live_rows[:, None], output_grad, jnp.zeros_like(output_grad))
    whole = lax.all_gather(masked, "tensor", axis=0, tiled=True)
    stores = (
        lax.all_gather(adapter_down, "dp", axis=0, tiled=True),
        lax.all_gather(adapter_up, "dp", axis=0, tiled=True),
    )
    choose = (seg_slot[:, None] == slot_ids[None, :]).astype(jnp.bfloat16)
    down_seg = jnp.dot(choose, stores[0].reshape(adapters, -1), preferred_element_type=jnp.float32)
    down_seg = down_seg.astype(jnp.bfloat16).reshape(seg_group, rank_dim, width_shard)
    up_seg = jnp.dot(choose, stores[1].reshape(adapters, -1), preferred_element_type=jnp.float32)
    up_seg = up_seg.astype(jnp.bfloat16).reshape(seg_group, rank_dim, key_shard)
    own_keys = lax.dynamic_slice_in_dim(whole, position * key_shard, key_shard, 1).reshape(
        seg_group, seg_len, key_shard
    )
    input_seg = layer_input.reshape(seg_group, seg_len, width_shard)
    up_part = jnp.einsum("sjk,srk->rsj", own_keys, up_seg, preferred_element_type=jnp.float32)
    down_part = jnp.einsum("sjd,srd->rsj", input_seg, down_seg, preferred_element_type=jnp.float32)
    lowrank, projected = lax.psum((up_part, down_part), "tensor")
    lowrank = lowrank.astype(jnp.bfloat16)
    projected = projected.astype(jnp.bfloat16)
    frozen = lax.dot_general(
        whole, key_weight, (((1,), (1,)), ((), ())), preferred_element_type=jnp.float32
    )
    extra = jnp.einsum("rsj,srd->sjd", lowrank, down_seg, preferred_element_type=jnp.float32)
    input_grad = (frozen + 2.0 * extra.reshape(tok_group, width_shard)).astype(jnp.bfloat16)
    seg_down = 2.0 * jnp.einsum(
        "rsj,sjd->srd", lowrank, input_seg, preferred_element_type=jnp.float32
    )
    seg_up = 2.0 * jnp.einsum(
        "rsj,sjk->srk", projected, own_keys, preferred_element_type=jnp.float32
    )
    seg_index = jnp.arange(seg_group, dtype=jnp.int32)
    same = seg_slot[:, None] == seg_slot[None, :]
    earlier = same & (seg_index[None, :] < seg_index[:, None])
    leading = jnp.logical_not(jnp.any(earlier, axis=1))
    merge_rows = (same & leading[:, None]).astype(jnp.float32)
    rows_down = jnp.einsum(
        "us,srd->urd", merge_rows, seg_down, precision=lax.Precision.HIGHEST
    ).astype(jnp.bfloat16)
    rows_up = jnp.einsum("us,srk->urk", merge_rows, seg_up, precision=lax.Precision.HIGHEST).astype(
        jnp.bfloat16
    )
    every_down, every_up = (
        lax.all_gather(rows_down, "dp", axis=0, tiled=True),
        lax.all_gather(rows_up, "dp", axis=0, tiled=True),
    )
    owned = group_index * per_owner + jnp.arange(per_owner, dtype=jnp.int32)
    mine = (every_slot[:, None] == owned[None, :]).astype(jnp.bfloat16)
    down_grad = jnp.einsum(
        "sp,srd->prd", mine, every_down, preferred_element_type=jnp.float32
    ).astype(jnp.bfloat16)
    up_grad = jnp.einsum("sp,srk->prk", mine, every_up, preferred_element_type=jnp.float32).astype(
        jnp.bfloat16
    )
    return (input_grad, down_grad, up_grad)


def device_program(layer_input, output_grad, key_weight, adapter_down, adapter_up, segment_adapter, adapter_slot, live_segments):
    args = (layer_input, output_grad, key_weight, adapter_down, adapter_up, segment_adapter, adapter_slot, live_segments)
    seg_group = segment_adapter.shape[0] // lax.axis_size("dp")
    one_each = seg_group == lax.axis_size("tensor")
    tiled = adapter_up.shape[2] % 128 == 0 and layer_input.shape[1] % 256 == 0
    if one_each and tiled and lax.axis_size("dp") % 2 == 0:
        return fused(*args)
    return on_device(*args)


def solution(mesh):
    in_specs = (
        P("dp", "tensor"),
        P(("dp", "tensor"), None),
        P("tensor", None),
        P("dp", None, "tensor"),
        P("dp", None, "tensor"),
        P(),
        P(),
        P("dp"),
    )
    out_specs = (P("dp", "tensor"), P("dp", None, "tensor"), P("dp", None, "tensor"))
    return jax.shard_map(
        device_program, mesh=mesh, in_specs=in_specs, out_specs=out_specs, check_vma=False
    )
```

```python
import functools

import jax
import jax.numpy as jnp
from jax import lax
from jax.experimental import pallas as pl
from jax.experimental.pallas import tpu as pltpu
from jax.sharding import PartitionSpec as P

MESH = pl.DeviceIdType.MESH
CHUNKS = 4
VMEM_LIMIT = 62 * 1024 * 1024
NT = (((1,), (1,)), ((), ()))
TN = (((0,), (0,)), ((), ()))


def fused_kernel(
    dims,
    adapter_hbm, slot_hbm, live_hbm,
    x_hbm, og_hbm, kw_hbm, ad_hbm, au_hbm,
    ig_hbm, dg_hbm, ug_hbm,
    adapter_s, slot_s, live_s, seg_slot, first,
    x_v, kw_v, ad_v, au_v, og_v, whole, ig_v, dg_v, ug_v,
    s1d_out, s1d_in, s2d_out, s2d_in, fu_out, fu_in,
    down_seg, up_seg, up_own, lr, pr_out, pr_in, su_out, su_in, rows_d, rows_u,
    load_sem, store_sem, blk_send, blk_recv, s1_send, s1_recv, s2_send, s2_recv, fu_send, fu_recv,
    up_send, up_recv, lr_send, lr_recv, pr_send, pr_recv, su_send, su_recv,
    rwy_send, rwu_send, rwc_send, rw_recv,
):
    T, X, Q, S, L, R, W, K, KS, PO = dims
    Z, Y = T // X, Q // 2
    half = L // CHUNKS
    t, q = lax.axis_index("tensor"), lax.axis_index("dp")
    z, x = t // X, lax.rem(t, X)
    y, c = q // 2, lax.rem(q, 2)
    mate = q + 1 - 2 * c
    pending = []

    def send(src, dst, send_sem, recv_sem, to, when=None):
        copy = pltpu.make_async_remote_copy(
            src_ref=src, dst_ref=dst, send_sem=send_sem, recv_sem=recv_sem,
            device_id=to, device_id_type=MESH,
        )
        if when is None:
            copy.start()
        else:
            pl.when(when)(copy.start)
        pending.append((when, copy))

    def arrived(ref, sem, when=None):
        copy = pltpu.make_async_copy(ref, ref, sem)
        if when is None:
            copy.wait()
        else:
            pl.when(when)(copy.wait)

    scalars = [
        pltpu.make_async_copy(adapter_hbm, adapter_s, load_sem.at[5]),
        pltpu.make_async_copy(slot_hbm, slot_s, load_sem.at[6]),
        pltpu.make_async_copy(live_hbm, live_s, load_sem.at[7]),
    ]
    loads = [
        pltpu.make_async_copy(og_hbm, og_v, load_sem.at[0]),
        pltpu.make_async_copy(au_hbm, au_v, load_sem.at[2]),
        pltpu.make_async_copy(ad_hbm, ad_v, load_sem.at[1]),
    ]
    later_loads = [
        pltpu.make_async_copy(x_hbm, x_v, load_sem.at[3]),
        pltpu.make_async_copy(kw_hbm, kw_v, load_sem.at[4]),
    ]
    for copy in scalars + loads:
        copy.start()

    tensor_peers = [lax.rem(t + j, T) for j in range(1, T)]
    far = [lax.rem(y + j, Y) for j in range(1, Y)]
    barrier = pltpu.get_barrier_semaphore()
    for peer in tensor_peers:
        pl.semaphore_signal(barrier, inc=1, device_id={"tensor": peer}, device_id_type=MESH)
    dp_peers = [lax.rem(q + j, Q) for j in range(1, Q)]
    for peer in dp_peers:
        pl.semaphore_signal(barrier, inc=1, device_id={"dp": peer}, device_id_type=MESH)

    scalars[2].wait()
    loads[0].wait()
    live = t < live_s[0]
    own_rows = jnp.where(live, og_v[...], jnp.zeros((L, K), jnp.bfloat16))
    whole[t] = own_rows

    pl.semaphore_wait(barrier, T - 1 + Q - 1)

    def rows_of(origin, part):
        return whole.at[origin, pl.ds(part * half, half)]

    def to_z(origin, part, up, when):
        step = 1 if up else -1
        edge = (z + 1 < Z) if up else (z > 0)
        when = edge if when is None else jnp.logical_and(when, edge)
        ref = rows_of(origin, part)
        send(ref, ref, blk_send.at[origin, part, 0 if up else 1], blk_recv.at[origin, part],
             {"tensor": t + step * X}, when)

    def to_x(origin, part, when):
        ref = rows_of(origin, part)
        for j in range(1, X):
            to = z * X + lax.rem(x + j, X)
            send(ref, ref, blk_send.at[origin, part, 1 + j], blk_recv.at[origin, part],
                 {"tensor": to}, when)

    paired = X == 2 and Z % 2 == 0
    direct = CHUNKS // 2 if paired else CHUNKS
    pair_z = z + 1 - 2 * lax.rem(z, 2)
    column = z * X + lax.rem(x + 1, X)
    for part in range(CHUNKS):
        to_z(t, part, True, None)
        to_z(t, part, False, None)
        to_x(t, part, None)

    def forward(step, part):
        for sign in (-1, 1):
            row = z + sign * step
            inside = jnp.logical_and(row >= 0, row < Z)
            origin = jnp.where(inside, row, z) * X + x
            arrived(rows_of(origin, part), blk_recv.at[origin, part], inside)
            to_z(origin, part, sign < 0, inside)
            across = inside
            if part >= direct:
                across = jnp.logical_and(inside, row != pair_z)
            to_x(origin, part, across)

    def share(part):
        if paired:
            ref = rows_of(column, part)
            arrived(ref, blk_recv.at[column, part])
            send(ref, ref, blk_send.at[column, part, 0], blk_recv.at[column, part],
                 {"tensor": pair_z * X + x})

    for copy in scalars[:2]:
        copy.wait()
    for s in range(Q * S):
        seg_slot[s] = slot_s[adapter_s[s]]

    def owned(index):
        local = seg_slot[index] - q * PO
        inside = jnp.logical_and(local >= 0, local < PO)
        return inside, jnp.clip(local, 0, PO - 1)

    loads[1].wait()

    def choose_up(i, carry):
        group, s = i // S, lax.rem(i, S)
        inside, local = owned(i)
        fu_out[group, s] = jnp.where(inside, au_v[local], jnp.zeros((R, KS), jnp.bfloat16))
        return carry

    lax.fori_loop(0, Q * S, choose_up, 0)
    for peer in dp_peers:
        send(fu_out.at[peer], fu_in.at[q], fu_send.at[peer], fu_recv.at[q], {"dp": peer})

    loads[2].wait()

    def choose_down(i, carry):
        group, s = i // S, lax.rem(i, S)
        inside, local = owned((group * 2 + 1 - c) * S + s)
        s1d_out[group, s] = jnp.where(inside, ad_v[local], jnp.zeros((R, W), jnp.bfloat16))
        return carry

    lax.fori_loop(0, Y * S, choose_down, 0)
    for copy in later_loads:
        copy.start()
    send(s1d_out, s1d_in, s1_send.at[0], s1_recv.at[0], {"dp": mate})

    def first_of(p, carry):
        slot = q * PO + p
        for group in range(Q):
            index = jnp.int32(-1)
            for s in reversed(range(S)):
                index = jnp.where(seg_slot[group * S + s] == slot, jnp.int32(s), index)
            first[p * Q + group] = index
        return carry

    lax.fori_loop(0, PO, first_of, 0)

    def combine_down(i, carry):
        group, s = i // S, lax.rem(i, S)
        inside, local = owned((group * 2 + c) * S + s)
        s2d_out[group, s] = jnp.where(inside, ad_v[local], s1d_in[group, s])
        return carry

    arrived(s1d_in, s1_recv.at[0])
    lax.fori_loop(0, Y * S, combine_down, 0)
    for other in far:
        send(s2d_out.at[other], s2d_in.at[y], s2_send.at[other, 0], s2_recv.at[y, 0],
             {"dp": other * 2 + c})

    forward(1, 0)

    total = fu_out[q]
    for peer in dp_peers:
        arrived(fu_in.at[peer], fu_recv.at[peer])
        total = total + fu_in[peer]
    up_seg[...] = total
    for peer in tensor_peers:
        send(up_seg.at[peer], up_own.at[t], up_send.at[peer], up_recv.at[t], {"tensor": peer})
    up_own[t] = up_seg[t]

    forward(1, 1)
    forward(1, 2)

    for peer in tensor_peers:
        arrived(up_own.at[peer], up_recv.at[peer])
    acc = jnp.zeros((R, L), jnp.float32)
    for p in range(T):
        acc = acc + lax.dot_general(
            up_own[p], whole[t, :, p * KS:(p + 1) * KS], NT, preferred_element_type=jnp.float32
        )
    lr[t] = acc.astype(jnp.bfloat16)
    for peer in tensor_peers:
        send(lr.at[t], lr.at[t], lr_send.at[peer], lr_recv.at[t], {"tensor": peer})

    share(2)
    forward(1, 3)
    share(3)
    if Z > 2:
        forward(2, 0)

    for other in far:
        arrived(s2d_in.at[other], s2_recv.at[other, 0])
    later_loads[0].wait()

    def down_of(s, carry):
        rows = s2d_out[y, s]
        for other in far:
            rows = rows + s2d_in[other, s]
        down_seg[s] = rows
        pr_out[s] = lax.dot_general(rows, x_v[s], NT, preferred_element_type=jnp.float32)
        return carry

    lax.fori_loop(0, S, down_of, 0)
    for peer in tensor_peers:
        send(pr_out.at[peer], pr_in.at[t], pr_send.at[peer], pr_recv.at[t], {"tensor": peer})
    pr_in[t] = pr_out[t]

    if Z > 2:
        forward(2, 1)

    for peer in tensor_peers:
        arrived(lr.at[peer], lr_recv.at[peer])

    own_slots = [seg_slot[q * S + s] for s in range(S)]

    def merged(parts, u, zero):
        return [jnp.where(own_slots[u] == own_slots[s], parts[s], zero) for s in range(S)]

    zero_l = jnp.zeros((R, L), jnp.bfloat16)
    ranks = [lr[s] for s in range(S)]
    left = jnp.concatenate(
        [jnp.concatenate(merged(ranks, u, zero_l), axis=1) for u in range(S)], axis=0
    )
    tile = 256
    for n in range(W // tile):
        columns = slice(n * tile, (n + 1) * tile)
        right = jnp.concatenate([x_v[s, :, columns] for s in range(S)], axis=0)
        grad = 2.0 * jnp.dot(left, right, preferred_element_type=jnp.float32)
        rows_d[q, :, :, columns] = grad.astype(jnp.bfloat16).reshape(S, R, tile)
    for other in far:
        send(rows_d.at[q], rows_d.at[q], rwy_send.at[other], rw_recv.at[q, 0],
             {"dp": other * 2 + c})
    send(rows_d.at[q], rows_d.at[q], rwc_send.at[q], rw_recv.at[q, 0], {"dp": mate})

    if Z > 2:
        forward(2, 2)

    later_loads[1].wait()

    def block_row(row):
        left_rows = whole[pl.ds(row * X, X)].reshape(X * L, K)
        for n in range(W // tile):
            at = slice(n * tile, (n + 1) * tile)
            value = lax.dot_general(left_rows, kw_v[at, :], NT, preferred_element_type=jnp.float32)
            for j in range(X):
                origin = row * X + j
                extra = lax.dot_general(
                    lr[origin], down_seg[origin, :, at], TN, preferred_element_type=jnp.float32
                )
                ig_v[origin, :, at] = (value[j * L:(j + 1) * L] + 2.0 * extra).astype(jnp.bfloat16)
        rows = pl.ds(row * X, X)
        pltpu.make_async_copy(ig_v.at[rows], ig_hbm.at[rows], store_sem.at[row]).start()

    def wait_side(row, parts):
        for j in range(1, X):
            origin = row * X + lax.rem(x + j, X)
            for part in parts:
                arrived(rows_of(origin, part), blk_recv.at[origin, part])

    def nearest(i):
        low, high = z, Z - 1 - z
        both = jnp.minimum(low, high)
        near = z + (-1 if i % 2 else 1) * ((i + 1) // 2)
        beyond = jnp.where(low < high, z + (i - both), z - (i - both))
        return jnp.where(i <= 2 * both, near, beyond)

    wait_side(z, range(direct))
    block_row(z)
    if Z > 2:
        forward(2, 3)

    for peer in tensor_peers:
        arrived(pr_in.at[peer], pr_recv.at[peer])
    acc = pr_in[0]
    for p in range(1, T):
        acc = acc + pr_in[p]
    projected = acc.astype(jnp.bfloat16)
    for p in range(T):
        su_out[p] = 2.0 * jnp.dot(
            projected, whole[t, :, p * KS:(p + 1) * KS], preferred_element_type=jnp.float32
        )
    for peer in tensor_peers:
        send(su_out.at[peer], su_in.at[t], su_send.at[peer], su_recv.at[t], {"tensor": peer})
    su_in[t] = su_out[t]

    for step in range(3, Z):
        forward(step, 0)
    wait_side(nearest(1), range(CHUNKS))
    block_row(nearest(1))
    for step in range(3, Z):
        forward(step, 1)

    for peer in tensor_peers:
        arrived(su_in.at[peer], su_recv.at[peer])
    zero_u = jnp.zeros((R, KS), jnp.float32)
    for u in range(S):
        total = zero_u
        for s in range(S):
            total = total + jnp.where(own_slots[u] == own_slots[s], su_in[s], zero_u)
        rows_u[q, u] = total.astype(jnp.bfloat16)
    for peer in dp_peers:
        send(rows_u.at[q], rows_u.at[q], rwu_send.at[peer], rw_recv.at[q, 1], {"dp": peer})

    for i in range(2, Z - 1):
        wait_side(nearest(i), range(CHUNKS))
        block_row(nearest(i))
    for step in range(3, Z):
        forward(step, 2)
    for other in far:
        origin = other * 2 + c
        arrived(rows_d.at[origin], rw_recv.at[origin, 0])
        send(rows_d.at[origin], rows_d.at[origin], rwc_send.at[origin],
             rw_recv.at[origin, 0], {"dp": mate})
    for step in range(3, Z):
        forward(step, 3)

    for group in range(Y):
        origin = group * 2 + 1 - c
        arrived(rows_d.at[origin], rw_recv.at[origin, 0])
    for peer in dp_peers:
        arrived(rows_u.at[peer], rw_recv.at[peer, 1])

    def owner_rows(p, carry):
        down_total = jnp.zeros((R, W), jnp.float32)
        up_total = jnp.zeros((R, KS), jnp.float32)
        for group in range(Q):
            index = first[p * Q + group]
            has = index >= 0
            index = jnp.maximum(index, 0)
            down_total += jnp.where(has, rows_d[group, index].astype(jnp.float32), 0.0)
            up_total += jnp.where(has, rows_u[group, index].astype(jnp.float32), 0.0)
        dg_v[p] = down_total.astype(jnp.bfloat16)
        ug_v[p] = up_total.astype(jnp.bfloat16)
        return carry

    lax.fori_loop(0, PO, owner_rows, 0, unroll=2)
    stores = [
        pltpu.make_async_copy(dg_v, dg_hbm, store_sem.at[Z]),
        pltpu.make_async_copy(ug_v, ug_hbm, store_sem.at[Z + 1]),
    ]
    for copy in stores:
        copy.start()

    if Z > 2:
        wait_side(nearest(Z - 1), range(CHUNKS))
        block_row(nearest(Z - 1))

    for when, copy in pending:
        if when is None:
            copy.wait_send()
        else:
            pl.when(when)(copy.wait_send)
    for row in range(Z):
        rows = pl.ds(row * X, X)
        pltpu.make_async_copy(ig_v.at[rows], ig_hbm.at[rows], store_sem.at[row]).wait()
    for copy in stores:
        copy.wait()


def store_kernel(a, b, c, a_out, b_out, c_out, sem):
    copies = [pltpu.make_async_copy(c, c_out, sem.at[0])]
    for src, dst, pieces in ((a, a_out, 4), (b, b_out, 2)):
        count = src.shape[0] // pieces
        for i in range(pieces):
            at = pl.ds(i * count, count)
            copies.append(pltpu.make_async_copy(src.at[at], dst.at[at], sem.at[len(copies)]))
    for copy in copies:
        copy.start()
    for copy in copies:
        copy.wait()


def fused(layer_input, output_grad, key_weight, adapter_down, adapter_up, segment_adapter, adapter_slot, live_segments):
    T, Q = lax.axis_size("tensor"), lax.axis_size("dp")
    X = 1 << ((T.bit_length() - 1) // 2)
    W = layer_input.shape[1]
    L, K = output_grad.shape
    PO, R, KS = adapter_up.shape
    S = segment_adapter.shape[0] // Q
    Y = Q // 2
    dims = (T, X, Q, S, L, R, W, K, KS, PO)
    bf, f32 = jnp.bfloat16, jnp.float32
    V, DMA = pltpu.VMEM, pltpu.SemaphoreType.DMA
    far_in = pl.BlockSpec(memory_space=pltpu.HBM)
    hbm = pl.BlockSpec(memory_space=pl.ANY)
    flops = 2 * T * L * K * W + 8 * T * L * R * W
    input_grad, down_grad, up_grad = pl.pallas_call(
        functools.partial(fused_kernel, dims),
        out_shape=(
            jax.ShapeDtypeStruct((T, L, W), bf),
            jax.ShapeDtypeStruct((PO, R, W), bf),
            jax.ShapeDtypeStruct((PO, R, KS), bf),
        ),
        in_specs=[far_in] * 8,
        out_specs=(hbm,) * 3,
        scratch_shapes=[
            pltpu.SMEM((Q * S,), jnp.int32), pltpu.SMEM((adapter_slot.shape[0],), jnp.int32),
            pltpu.SMEM((1,), jnp.int32), pltpu.SMEM((Q * S,), jnp.int32),
            pltpu.SMEM((PO * Q,), jnp.int32),
            V((T, L, W), bf), V((W, K), bf), V((PO, R, W), bf), V((PO, R, KS), bf), V((L, K), bf),
            V((T, L, K), bf), V((T, L, W), bf), V((PO, R, W), bf), V((PO, R, KS), bf),
            V((Y, S, R, W), bf), V((Y, S, R, W), bf), V((Y, S, R, W), bf), V((Y, S, R, W), bf),
            V((Q, S, R, KS), bf), V((Q, S, R, KS), bf),
            V((S, R, W), bf), V((S, R, KS), bf), V((T, R, KS), bf), V((T, R, L), bf),
            V((S, R, L), f32), V((T, R, L), f32), V((T, R, KS), f32), V((T, R, KS), f32),
            V((Q, S, R, W), bf), V((Q, S, R, KS), bf),
            DMA((8,)), DMA((T + 2,)), DMA((T, CHUNKS, 1 + X)), DMA((T, CHUNKS)),
            DMA((2,)), DMA((2,)), DMA((Y, 2)), DMA((Y, 2)), DMA((Q,)), DMA((Q,)),
            DMA((T,)), DMA((T,)), DMA((T,)), DMA((T,)),
            DMA((T,)), DMA((T,)), DMA((T,)), DMA((T,)),
            DMA((Y,)), DMA((Q,)), DMA((Q,)), DMA((Q, 2)),
        ],
        compiler_params=pltpu.CompilerParams(
            collective_id=0, has_side_effects=True, vmem_limit_bytes=VMEM_LIMIT
        ),
        cost_estimate=pl.CostEstimate(
            flops=flops, bytes_accessed=2 * (2 * T * L * W + K * W + 2 * PO * R * W), transcendentals=0
        ),
    )(
        segment_adapter, adapter_slot, live_segments,
        layer_input.reshape(T, L, W), output_grad, key_weight, adapter_down, adapter_up,
    )
    results = (input_grad, down_grad, up_grad)
    input_grad, down_grad, up_grad = pl.pallas_call(
        store_kernel,
        out_shape=tuple(jax.ShapeDtypeStruct(r.shape, r.dtype) for r in results),
        in_specs=[hbm] * 3,
        out_specs=(hbm,) * 3,
        scratch_shapes=[DMA((7,))],
        compiler_params=pltpu.CompilerParams(vmem_limit_bytes=VMEM_LIMIT),
        cost_estimate=pl.CostEstimate(
            flops=0, bytes_accessed=4 * (T * L * W + PO * R * W), transcendentals=0
        ),
    )(*results)
    return input_grad.reshape(T * L, W), down_grad, up_grad


def on_device(
    layer_input,
    output_grad,
    key_weight,
    adapter_down,
    adapter_up,
    segment_adapter,
    adapter_slot,
    live_segments,
):
    tensor_size = lax.axis_size("tensor")
    position = lax.axis_index("tensor")
    group_count = lax.axis_size("dp")
    group_index = lax.axis_index("dp")
    row_count = output_grad.shape[0]
    tok_group = layer_input.shape[0]
    width_shard = layer_input.shape[1]
    key_width = output_grad.shape[1]
    key_shard = key_width // tensor_size
    adapters = adapter_slot.shape[0]
    rank_dim = adapter_down.shape[1]
    seg_total = segment_adapter.shape[0]
    seg_group = seg_total // group_count
    seg_len = tok_group // seg_group
    per_owner = adapters // group_count
    slot_ids = jnp.arange(adapters, dtype=jnp.int32)
    lookup = segment_adapter[:, None] == slot_ids[None, :]
    every_slot = jnp.sum(jnp.where(lookup, adapter_slot[None, :], 0), axis=1)
    seg_slot = lax.dynamic_slice_in_dim(every_slot, group_index * seg_group, seg_group)
    local_rows = position * row_count + jnp.arange(row_count, dtype=jnp.int32)
    live_rows = local_rows // seg_len < live_segments[0]
    masked = jnp.where(live_rows[:, None], output_grad, jnp.zeros_like(output_grad))
    whole = lax.all_gather(masked, "tensor", axis=0, tiled=True)
    stores = (
        lax.all_gather(adapter_down, "dp", axis=0, tiled=True),
        lax.all_gather(adapter_up, "dp", axis=0, tiled=True),
    )
    choose = (seg_slot[:, None] == slot_ids[None, :]).astype(jnp.bfloat16)
    down_seg = jnp.dot(choose, stores[0].reshape(adapters, -1), preferred_element_type=jnp.float32)
    down_seg = down_seg.astype(jnp.bfloat16).reshape(seg_group, rank_dim, width_shard)
    up_seg = jnp.dot(choose, stores[1].reshape(adapters, -1), preferred_element_type=jnp.float32)
    up_seg = up_seg.astype(jnp.bfloat16).reshape(seg_group, rank_dim, key_shard)
    own_keys = lax.dynamic_slice_in_dim(whole, position * key_shard, key_shard, 1).reshape(
        seg_group, seg_len, key_shard
    )
    input_seg = layer_input.reshape(seg_group, seg_len, width_shard)
    up_part = jnp.einsum("sjk,srk->rsj", own_keys, up_seg, preferred_element_type=jnp.float32)
    down_part = jnp.einsum("sjd,srd->rsj", input_seg, down_seg, preferred_element_type=jnp.float32)
    lowrank, projected = lax.psum((up_part, down_part), "tensor")
    lowrank = lowrank.astype(jnp.bfloat16)
    projected = projected.astype(jnp.bfloat16)
    frozen = lax.dot_general(
        whole, key_weight, (((1,), (1,)), ((), ())), preferred_element_type=jnp.float32
    )
    extra = jnp.einsum("rsj,srd->sjd", lowrank, down_seg, preferred_element_type=jnp.float32)
    input_grad = (frozen + 2.0 * extra.reshape(tok_group, width_shard)).astype(jnp.bfloat16)
    seg_down = 2.0 * jnp.einsum(
        "rsj,sjd->srd", lowrank, input_seg, preferred_element_type=jnp.float32
    )
    seg_up = 2.0 * jnp.einsum(
        "rsj,sjk->srk", projected, own_keys, preferred_element_type=jnp.float32
    )
    seg_index = jnp.arange(seg_group, dtype=jnp.int32)
    same = seg_slot[:, None] == seg_slot[None, :]
    earlier = same & (seg_index[None, :] < seg_index[:, None])
    leading = jnp.logical_not(jnp.any(earlier, axis=1))
    merge_rows = (same & leading[:, None]).astype(jnp.float32)
    rows_down = jnp.einsum(
        "us,srd->urd", merge_rows, seg_down, precision=lax.Precision.HIGHEST
    ).astype(jnp.bfloat16)
    rows_up = jnp.einsum("us,srk->urk", merge_rows, seg_up, precision=lax.Precision.HIGHEST).astype(
        jnp.bfloat16
    )
    every_down, every_up = (
        lax.all_gather(rows_down, "dp", axis=0, tiled=True),
        lax.all_gather(rows_up, "dp", axis=0, tiled=True),
    )
    owned = group_index * per_owner + jnp.arange(per_owner, dtype=jnp.int32)
    mine = (every_slot[:, None] == owned[None, :]).astype(jnp.bfloat16)
    down_grad = jnp.einsum(
        "sp,srd->prd", mine, every_down, preferred_element_type=jnp.float32
    ).astype(jnp.bfloat16)
    up_grad = jnp.einsum("sp,srk->prk", mine, every_up, preferred_element_type=jnp.float32).astype(
        jnp.bfloat16
    )
    return (input_grad, down_grad, up_grad)


def device_program(layer_input, output_grad, key_weight, adapter_down, adapter_up, segment_adapter, adapter_slot, live_segments):
    args = (layer_input, output_grad, key_weight, adapter_down, adapter_up, segment_adapter, adapter_slot, live_segments)
    seg_group = segment_adapter.shape[0] // lax.axis_size("dp")
    one_each = seg_group == lax.axis_size("tensor")
    tiled = adapter_up.shape[2] % 128 == 0 and layer_input.shape[1] % 256 == 0
    if one_each and tiled and lax.axis_size("dp") % 2 == 0:
        return fused(*args)
    return on_device(*args)


def solution(mesh):
    in_specs = (
        P("dp", "tensor"),
        P(("dp", "tensor"), None),
        P("tensor", None),
        P("dp", None, "tensor"),
        P("dp", None, "tensor"),
        P(),
        P(),
        P("dp"),
    )
    out_specs = (P("dp", "tensor"), P("dp", None, "tensor"), P("dp", None, "tensor"))
    return jax.shard_map(
        device_program, mesh=mesh, in_specs=in_specs, out_specs=out_specs, check_vma=False
    )
```

```python
import functools

import jax
import jax.numpy as jnp
from jax import lax
from jax.experimental import pallas as pl
from jax.experimental.pallas import tpu as pltpu
from jax.sharding import PartitionSpec as P

MESH = pl.DeviceIdType.MESH
CHUNKS = 4
VMEM_LIMIT = 62 * 1024 * 1024
NT = (((1,), (1,)), ((), ()))
TN = (((0,), (0,)), ((), ()))


def fused_kernel(
    dims,
    adapter_hbm, slot_hbm, live_hbm,
    x_hbm, og_hbm, kw_hbm, ad_hbm, au_hbm,
    ig_hbm, dg_hbm, ug_hbm,
    adapter_s, slot_s, live_s, seg_slot, first,
    x_v, kw_v, ad_v, au_v, og_v, whole, ig_v, dg_v, ug_v,
    s1d_out, s1d_in, s2d_out, s2d_in, fu_out, fu_in,
    down_seg, up_seg, up_own, lr, pr_out, pr_in, su_out, su_in, rows_d, rows_u,
    load_sem, store_sem, blk_send, blk_recv, s1_send, s1_recv, s2_send, s2_recv, fu_send, fu_recv,
    up_send, up_recv, lr_send, lr_recv, pr_send, pr_recv, su_send, su_recv,
    rwy_send, rwu_send, rwc_send, rw_recv,
):
    T, X, Q, S, L, R, W, K, KS, PO = dims
    Z, Y = T // X, Q // 2
    half = L // CHUNKS
    t, q = lax.axis_index("tensor"), lax.axis_index("dp")
    z, x = t // X, lax.rem(t, X)
    y, c = q // 2, lax.rem(q, 2)
    mate = q + 1 - 2 * c
    pending = []

    def send(src, dst, send_sem, recv_sem, to, when=None):
        copy = pltpu.make_async_remote_copy(
            src_ref=src, dst_ref=dst, send_sem=send_sem, recv_sem=recv_sem,
            device_id=to, device_id_type=MESH,
        )
        if when is None:
            copy.start()
        else:
            pl.when(when)(copy.start)
        pending.append((when, copy))

    def arrived(ref, sem, when=None):
        copy = pltpu.make_async_copy(ref, ref, sem)
        if when is None:
            copy.wait()
        else:
            pl.when(when)(copy.wait)

    scalars = [
        pltpu.make_async_copy(adapter_hbm, adapter_s, load_sem.at[5]),
        pltpu.make_async_copy(slot_hbm, slot_s, load_sem.at[6]),
        pltpu.make_async_copy(live_hbm, live_s, load_sem.at[7]),
    ]
    loads = [
        pltpu.make_async_copy(og_hbm, og_v, load_sem.at[0]),
        pltpu.make_async_copy(au_hbm, au_v, load_sem.at[2]),
        pltpu.make_async_copy(ad_hbm, ad_v, load_sem.at[1]),
    ]
    later_loads = [
        pltpu.make_async_copy(x_hbm, x_v, load_sem.at[3]),
        pltpu.make_async_copy(kw_hbm, kw_v, load_sem.at[4]),
    ]
    for copy in scalars + loads:
        copy.start()

    tensor_peers = [lax.rem(t + j, T) for j in range(1, T)]
    far = [lax.rem(y + j, Y) for j in range(1, Y)]
    barrier = pltpu.get_barrier_semaphore()
    for peer in tensor_peers:
        pl.semaphore_signal(barrier, inc=1, device_id={"tensor": peer}, device_id_type=MESH)
    dp_peers = [lax.rem(q + j, Q) for j in range(1, Q)]
    for peer in dp_peers:
        pl.semaphore_signal(barrier, inc=1, device_id={"dp": peer}, device_id_type=MESH)

    for copy in scalars[:2]:
        copy.wait()
    for s in range(Q * S):
        seg_slot[s] = slot_s[adapter_s[s]]

    def owned(index):
        local = seg_slot[index] - q * PO
        inside = jnp.logical_and(local >= 0, local < PO)
        return inside, jnp.clip(local, 0, PO - 1)

    loads[2].wait()

    def choose_down(i, carry):
        group, s = i // S, lax.rem(i, S)
        inside, local = owned((group * 2 + 1 - c) * S + s)
        s1d_out[group, s] = jnp.where(inside, ad_v[local], jnp.zeros((R, W), jnp.bfloat16))
        return carry

    lax.fori_loop(0, Y * S, choose_down, 0)
    loads[1].wait()

    def choose_up(i, carry):
        group, s = i // S, lax.rem(i, S)
        inside, local = owned(i)
        fu_out[group, s] = jnp.where(inside, au_v[local], jnp.zeros((R, KS), jnp.bfloat16))
        return carry

    lax.fori_loop(0, Q * S, choose_up, 0)
    pl.semaphore_wait(barrier, T - 1 + Q - 1)

    for copy in later_loads:
        copy.start()
    send(s1d_out, s1d_in, s1_send.at[0], s1_recv.at[0], {"dp": mate})

    for peer in dp_peers:
        send(fu_out.at[peer], fu_in.at[q], fu_send.at[peer], fu_recv.at[q], {"dp": peer})

    scalars[2].wait()
    loads[0].wait()
    live = t < live_s[0]
    own_rows = jnp.where(live, og_v[...], jnp.zeros((L, K), jnp.bfloat16))
    whole[t] = own_rows

    def rows_of(origin, part):
        return whole.at[origin, pl.ds(part * half, half)]

    def to_z(origin, part, up, when):
        step = 1 if up else -1
        edge = (z + 1 < Z) if up else (z > 0)
        when = edge if when is None else jnp.logical_and(when, edge)
        ref = rows_of(origin, part)
        send(ref, ref, blk_send.at[origin, part, 0 if up else 1], blk_recv.at[origin, part],
             {"tensor": t + step * X}, when)

    def to_x(origin, part, when):
        ref = rows_of(origin, part)
        for j in range(1, X):
            to = z * X + lax.rem(x + j, X)
            send(ref, ref, blk_send.at[origin, part, 1 + j], blk_recv.at[origin, part],
                 {"tensor": to}, when)

    paired = X == 2 and Z % 2 == 0
    direct = CHUNKS // 2 if paired else CHUNKS
    pair_z = z + 1 - 2 * lax.rem(z, 2)
    column = z * X + lax.rem(x + 1, X)
    def start_own(part):
        to_z(t, part, True, None)
        to_z(t, part, False, None)
        to_x(t, part, None)

    start_own(0)

    def forward(step, part):
        for sign in (-1, 1):
            row = z + sign * step
            inside = jnp.logical_and(row >= 0, row < Z)
            origin = jnp.where(inside, row, z) * X + x
            arrived(rows_of(origin, part), blk_recv.at[origin, part], inside)
            to_z(origin, part, sign < 0, inside)
            across = inside
            if part >= direct:
                across = jnp.logical_and(inside, row != pair_z)
            to_x(origin, part, across)

    def share(part):
        if paired:
            ref = rows_of(column, part)
            arrived(ref, blk_recv.at[column, part])
            send(ref, ref, blk_send.at[column, part, 0], blk_recv.at[column, part],
                 {"tensor": pair_z * X + x})

    def combine_down(i, carry):
        group, s = i // S, lax.rem(i, S)
        inside, local = owned((group * 2 + c) * S + s)
        s2d_out[group, s] = jnp.where(inside, ad_v[local], s1d_in[group, s])
        return carry

    def first_of(p, carry):
        slot = q * PO + p
        for group in range(Q):
            index = jnp.int32(-1)
            for s in reversed(range(S)):
                index = jnp.where(seg_slot[group * S + s] == slot, jnp.int32(s), index)
            first[p * Q + group] = index
        return carry

    lax.fori_loop(0, PO, first_of, 0)

    arrived(s1d_in, s1_recv.at[0])
    part_segs = S // 2

    def segs(piece):
        return pl.ds(piece * part_segs, part_segs)

    for piece in range(2):
        def combine_piece(i, carry):
            return combine_down(i // part_segs * S + piece * part_segs + lax.rem(i, part_segs), carry)

        lax.fori_loop(0, Y * part_segs, combine_piece, 0)
        for other in far:
            send(s2d_out.at[other, segs(piece)], s2d_in.at[y, segs(piece)], s2_send.at[other, piece],
                 s2_recv.at[y, piece], {"dp": other * 2 + c})
    start_own(1)

    total = fu_out[q]
    for peer in dp_peers:
        arrived(fu_in.at[peer], fu_recv.at[peer])
        total = total + fu_in[peer]
    up_seg[...] = total
    for peer in tensor_peers:
        send(up_seg.at[peer], up_own.at[t], up_send.at[peer], up_recv.at[t], {"tensor": peer})
    up_own[t] = up_seg[t]

    start_own(2)
    forward(1, 0)

    for peer in tensor_peers:
        arrived(up_own.at[peer], up_recv.at[peer])
    acc = jnp.zeros((R, L), jnp.float32)
    for p in range(T):
        acc = acc + lax.dot_general(
            up_own[p], whole[t, :, p * KS:(p + 1) * KS], NT, preferred_element_type=jnp.float32
        )
    lr[t] = acc.astype(jnp.bfloat16)
    for peer in tensor_peers:
        send(lr.at[t], lr.at[t], lr_send.at[peer], lr_recv.at[t], {"tensor": peer})

    start_own(3)
    forward(1, 1)
    share(2)
    forward(1, 2)

    later_loads[0].wait()

    def down_of(s, carry):
        rows = s2d_out[y, s]
        for other in far:
            rows = rows + s2d_in[other, s]
        down_seg[s] = rows
        pr_out[s] = lax.dot_general(rows, x_v[s], NT, preferred_element_type=jnp.float32)
        return carry

    def project(piece):
        for other in far:
            arrived(s2d_in.at[other, segs(piece)], s2_recv.at[other, piece])
        lax.fori_loop(piece * part_segs, (piece + 1) * part_segs, down_of, 0, unroll=2)
        for s in range(piece * part_segs, (piece + 1) * part_segs):
            remote = s != t
            send(pr_out.at[s], pr_in.at[t], pr_send.at[s], pr_recv.at[t], {"tensor": s}, remote)

            @pl.when(s == t)
            def _():
                pr_in[t] = pr_out[s]

    project(0)
    forward(1, 3)
    share(3)

    for peer in tensor_peers:
        arrived(lr.at[peer], lr_recv.at[peer])

    own_slots = [seg_slot[q * S + s] for s in range(S)]

    def merged(parts, u, zero):
        return [jnp.where(own_slots[u] == own_slots[s], parts[s], zero) for s in range(S)]

    zero_l = jnp.zeros((R, L), jnp.bfloat16)
    ranks = [lr[s] for s in range(S)]
    left = jnp.concatenate(
        [jnp.concatenate(merged(ranks, u, zero_l), axis=1) for u in range(S)], axis=0
    )
    tile = 256
    for n in range(W // tile):
        columns = slice(n * tile, (n + 1) * tile)
        right = jnp.concatenate([x_v[s, :, columns] for s in range(S)], axis=0)
        grad = 2.0 * jnp.dot(left, right, preferred_element_type=jnp.float32)
        rows_d[q, :, :, columns] = grad.astype(jnp.bfloat16).reshape(S, R, tile)
    for other in far:
        send(rows_d.at[q], rows_d.at[q], rwy_send.at[other], rw_recv.at[q, 0],
             {"dp": other * 2 + c})
    send(rows_d.at[q], rows_d.at[q], rwc_send.at[q], rw_recv.at[q, 0], {"dp": mate})

    if Z > 2:
        forward(2, 0)
    project(1)
    if Z > 2:
        forward(2, 1)
    if Z > 2:
        forward(2, 2)

    later_loads[1].wait()

    def block_row(row):
        left_rows = whole[pl.ds(row * X, X)].reshape(X * L, K)
        for n in range(W // tile):
            at = slice(n * tile, (n + 1) * tile)
            value = lax.dot_general(left_rows, kw_v[at, :], NT, preferred_element_type=jnp.float32)
            for j in range(X):
                origin = row * X + j
                extra = lax.dot_general(
                    lr[origin], down_seg[origin, :, at], TN, preferred_element_type=jnp.float32
                )
                ig_v[origin, :, at] = (value[j * L:(j + 1) * L] + 2.0 * extra).astype(jnp.bfloat16)
        rows = pl.ds(row * X, X)
        pltpu.make_async_copy(ig_v.at[rows], ig_hbm.at[rows], store_sem.at[row]).start()

    def wait_side(row, parts):
        for j in range(1, X):
            origin = row * X + lax.rem(x + j, X)
            for part in parts:
                arrived(rows_of(origin, part), blk_recv.at[origin, part])

    def nearest(i):
        low, high = z, Z - 1 - z
        both = jnp.minimum(low, high)
        near = z + (-1 if i % 2 else 1) * ((i + 1) // 2)
        beyond = jnp.where(low < high, z + (i - both), z - (i - both))
        return jnp.where(i <= 2 * both, near, beyond)

    wait_side(z, range(direct))
    block_row(z)
    if Z > 2:
        forward(2, 3)

    for peer in tensor_peers:
        arrived(pr_in.at[peer], pr_recv.at[peer])
    acc = pr_in[0]
    for p in range(1, T):
        acc = acc + pr_in[p]
    projected = acc.astype(jnp.bfloat16)
    for p in range(T):
        su_out[p] = 2.0 * jnp.dot(
            projected, whole[t, :, p * KS:(p + 1) * KS], preferred_element_type=jnp.float32
        )
    for peer in tensor_peers:
        send(su_out.at[peer], su_in.at[t], su_send.at[peer], su_recv.at[t], {"tensor": peer})
    su_in[t] = su_out[t]

    for step in range(3, Z):
        forward(step, 0)
    wait_side(nearest(1), range(CHUNKS))
    block_row(nearest(1))
    for step in range(3, Z):
        forward(step, 1)

    for peer in tensor_peers:
        arrived(su_in.at[peer], su_recv.at[peer])
    zero_u = jnp.zeros((R, KS), jnp.float32)
    for u in range(S):
        total = zero_u
        for s in range(S):
            total = total + jnp.where(own_slots[u] == own_slots[s], su_in[s], zero_u)
        rows_u[q, u] = total.astype(jnp.bfloat16)
    for peer in dp_peers:
        send(rows_u.at[q], rows_u.at[q], rwu_send.at[peer], rw_recv.at[q, 1], {"dp": peer})

    for i in range(2, Z - 1):
        wait_side(nearest(i), range(CHUNKS))
        block_row(nearest(i))
    for step in range(3, Z):
        forward(step, 2)
    for other in far:
        origin = other * 2 + c
        arrived(rows_d.at[origin], rw_recv.at[origin, 0])
        send(rows_d.at[origin], rows_d.at[origin], rwc_send.at[origin],
             rw_recv.at[origin, 0], {"dp": mate})
    for step in range(3, Z):
        forward(step, 3)

    for group in range(Y):
        origin = group * 2 + 1 - c
        arrived(rows_d.at[origin], rw_recv.at[origin, 0])

    def owner_sum(rows, out, p, width):
        total = jnp.zeros((R, width), jnp.float32)
        for group in range(Q):
            index = first[p * Q + group]
            row = rows[group, jnp.maximum(index, 0)].astype(jnp.float32)
            total += jnp.where(index >= 0, row, 0.0)
        out[p] = total.astype(jnp.bfloat16)

    def owner_down(p, carry):
        owner_sum(rows_d, dg_v, p, W)
        return carry

    def owner_up(p, carry):
        owner_sum(rows_u, ug_v, p, KS)
        return carry

    lax.fori_loop(0, PO, owner_down, 0, unroll=2)
    stores = [
        pltpu.make_async_copy(dg_v, dg_hbm, store_sem.at[Z]),
        pltpu.make_async_copy(ug_v, ug_hbm, store_sem.at[Z + 1]),
    ]
    stores[0].start()

    if Z > 2:
        wait_side(nearest(Z - 1), range(CHUNKS))
        block_row(nearest(Z - 1))

    for peer in dp_peers:
        arrived(rows_u.at[peer], rw_recv.at[peer, 1])
    lax.fori_loop(0, PO, owner_up, 0, unroll=4)
    stores[1].start()

    for when, copy in pending:
        if when is None:
            copy.wait_send()
        else:
            pl.when(when)(copy.wait_send)
    for row in range(Z):
        rows = pl.ds(row * X, X)
        pltpu.make_async_copy(ig_v.at[rows], ig_hbm.at[rows], store_sem.at[row]).wait()
    for copy in stores:
        copy.wait()


def store_kernel(a, b, c, a_out, b_out, c_out, a_v, b_v, c_v, in_sem, out_sem):
    moves = []
    for src, held, dst, pieces in ((a, a_v, a_out, 4), (b, b_v, b_out, 2), (c, c_v, c_out, 1)):
        count = src.shape[0] // pieces
        for i in range(pieces):
            at, n = pl.ds(i * count, count), len(moves)
            moves.append((
                pltpu.make_async_copy(src.at[at], held.at[at], in_sem.at[n]),
                pltpu.make_async_copy(held.at[at], dst.at[at], out_sem.at[n]),
            ))
    for load, _ in moves:
        load.start()
    for load, store in moves:
        load.wait()
        store.start()
    for _, store in moves:
        store.wait()


def fused(layer_input, output_grad, key_weight, adapter_down, adapter_up, segment_adapter, adapter_slot, live_segments):
    T, Q = lax.axis_size("tensor"), lax.axis_size("dp")
    X = 1 << ((T.bit_length() - 1) // 2)
    W = layer_input.shape[1]
    L, K = output_grad.shape
    PO, R, KS = adapter_up.shape
    S = segment_adapter.shape[0] // Q
    Y = Q // 2
    dims = (T, X, Q, S, L, R, W, K, KS, PO)
    bf, f32 = jnp.bfloat16, jnp.float32
    V, DMA = pltpu.VMEM, pltpu.SemaphoreType.DMA
    far_in = pl.BlockSpec(memory_space=pltpu.HBM)
    hbm = pl.BlockSpec(memory_space=pl.ANY)
    flops = 2 * T * L * K * W + 8 * T * L * R * W
    input_grad, down_grad, up_grad = pl.pallas_call(
        functools.partial(fused_kernel, dims),
        out_shape=(
            jax.ShapeDtypeStruct((T, L, W), bf),
            jax.ShapeDtypeStruct((PO, R, W), bf),
            jax.ShapeDtypeStruct((PO, R, KS), bf),
        ),
        in_specs=[far_in] * 8,
        out_specs=(hbm,) * 3,
        scratch_shapes=[
            pltpu.SMEM((Q * S,), jnp.int32), pltpu.SMEM((adapter_slot.shape[0],), jnp.int32),
            pltpu.SMEM((1,), jnp.int32), pltpu.SMEM((Q * S,), jnp.int32),
            pltpu.SMEM((PO * Q,), jnp.int32),
            V((T, L, W), bf), V((W, K), bf), V((PO, R, W), bf), V((PO, R, KS), bf), V((L, K), bf),
            V((T, L, K), bf), V((T, L, W), bf), V((PO, R, W), bf), V((PO, R, KS), bf),
            V((Y, S, R, W), bf), V((Y, S, R, W), bf), V((Y, S, R, W), bf), V((Y, S, R, W), bf),
            V((Q, S, R, KS), bf), V((Q, S, R, KS), bf),
            V((S, R, W), bf), V((S, R, KS), bf), V((T, R, KS), bf), V((T, R, L), bf),
            V((S, R, L), f32), V((T, R, L), f32), V((T, R, KS), f32), V((T, R, KS), f32),
            V((Q, S, R, W), bf), V((Q, S, R, KS), bf),
            DMA((8,)), DMA((T + 2,)), DMA((T, CHUNKS, 1 + X)), DMA((T, CHUNKS)),
            DMA((2,)), DMA((2,)), DMA((Y, 2)), DMA((Y, 2)), DMA((Q,)), DMA((Q,)),
            DMA((T,)), DMA((T,)), DMA((T,)), DMA((T,)),
            DMA((T,)), DMA((T,)), DMA((T,)), DMA((T,)),
            DMA((Y,)), DMA((Q,)), DMA((Q,)), DMA((Q, 2)),
        ],
        compiler_params=pltpu.CompilerParams(
            collective_id=0, has_side_effects=True, vmem_limit_bytes=VMEM_LIMIT
        ),
        cost_estimate=pl.CostEstimate(
            flops=flops, bytes_accessed=2 * (2 * T * L * W + K * W + 2 * PO * R * W), transcendentals=0
        ),
    )(
        segment_adapter, adapter_slot, live_segments,
        layer_input.reshape(T, L, W), output_grad, key_weight, adapter_down, adapter_up,
    )
    results = (input_grad, down_grad, up_grad)
    input_grad, down_grad, up_grad = pl.pallas_call(
        store_kernel,
        out_shape=tuple(jax.ShapeDtypeStruct(r.shape, r.dtype) for r in results),
        in_specs=[hbm] * 3,
        out_specs=(hbm,) * 3,
        scratch_shapes=[V(r.shape, r.dtype) for r in results] + [DMA((7,)), DMA((7,))],
        compiler_params=pltpu.CompilerParams(vmem_limit_bytes=VMEM_LIMIT),
        cost_estimate=pl.CostEstimate(
            flops=0, bytes_accessed=4 * (T * L * W + PO * R * W), transcendentals=0
        ),
    )(*results)
    return input_grad.reshape(T * L, W), down_grad, up_grad


def on_device(
    layer_input,
    output_grad,
    key_weight,
    adapter_down,
    adapter_up,
    segment_adapter,
    adapter_slot,
    live_segments,
):
    tensor_size = lax.axis_size("tensor")
    position = lax.axis_index("tensor")
    group_count = lax.axis_size("dp")
    group_index = lax.axis_index("dp")
    row_count = output_grad.shape[0]
    tok_group = layer_input.shape[0]
    width_shard = layer_input.shape[1]
    key_width = output_grad.shape[1]
    key_shard = key_width // tensor_size
    adapters = adapter_slot.shape[0]
    rank_dim = adapter_down.shape[1]
    seg_total = segment_adapter.shape[0]
    seg_group = seg_total // group_count
    seg_len = tok_group // seg_group
    per_owner = adapters // group_count
    slot_ids = jnp.arange(adapters, dtype=jnp.int32)
    lookup = segment_adapter[:, None] == slot_ids[None, :]
    every_slot = jnp.sum(jnp.where(lookup, adapter_slot[None, :], 0), axis=1)
    seg_slot = lax.dynamic_slice_in_dim(every_slot, group_index * seg_group, seg_group)
    local_rows = position * row_count + jnp.arange(row_count, dtype=jnp.int32)
    live_rows = local_rows // seg_len < live_segments[0]
    masked = jnp.where(live_rows[:, None], output_grad, jnp.zeros_like(output_grad))
    whole = lax.all_gather(masked, "tensor", axis=0, tiled=True)
    stores = (
        lax.all_gather(adapter_down, "dp", axis=0, tiled=True),
        lax.all_gather(adapter_up, "dp", axis=0, tiled=True),
    )
    choose = (seg_slot[:, None] == slot_ids[None, :]).astype(jnp.bfloat16)
    down_seg = jnp.dot(choose, stores[0].reshape(adapters, -1), preferred_element_type=jnp.float32)
    down_seg = down_seg.astype(jnp.bfloat16).reshape(seg_group, rank_dim, width_shard)
    up_seg = jnp.dot(choose, stores[1].reshape(adapters, -1), preferred_element_type=jnp.float32)
    up_seg = up_seg.astype(jnp.bfloat16).reshape(seg_group, rank_dim, key_shard)
    own_keys = lax.dynamic_slice_in_dim(whole, position * key_shard, key_shard, 1).reshape(
        seg_group, seg_len, key_shard
    )
    input_seg = layer_input.reshape(seg_group, seg_len, width_shard)
    up_part = jnp.einsum("sjk,srk->rsj", own_keys, up_seg, preferred_element_type=jnp.float32)
    down_part = jnp.einsum("sjd,srd->rsj", input_seg, down_seg, preferred_element_type=jnp.float32)
    lowrank, projected = lax.psum((up_part, down_part), "tensor")
    lowrank = lowrank.astype(jnp.bfloat16)
    projected = projected.astype(jnp.bfloat16)
    frozen = lax.dot_general(
        whole, key_weight, (((1,), (1,)), ((), ())), preferred_element_type=jnp.float32
    )
    extra = jnp.einsum("rsj,srd->sjd", lowrank, down_seg, preferred_element_type=jnp.float32)
    input_grad = (frozen + 2.0 * extra.reshape(tok_group, width_shard)).astype(jnp.bfloat16)
    seg_down = 2.0 * jnp.einsum(
        "rsj,sjd->srd", lowrank, input_seg, preferred_element_type=jnp.float32
    )
    seg_up = 2.0 * jnp.einsum(
        "rsj,sjk->srk", projected, own_keys, preferred_element_type=jnp.float32
    )
    seg_index = jnp.arange(seg_group, dtype=jnp.int32)
    same = seg_slot[:, None] == seg_slot[None, :]
    earlier = same & (seg_index[None, :] < seg_index[:, None])
    leading = jnp.logical_not(jnp.any(earlier, axis=1))
    merge_rows = (same & leading[:, None]).astype(jnp.float32)
    rows_down = jnp.einsum(
        "us,srd->urd", merge_rows, seg_down, precision=lax.Precision.HIGHEST
    ).astype(jnp.bfloat16)
    rows_up = jnp.einsum("us,srk->urk", merge_rows, seg_up, precision=lax.Precision.HIGHEST).astype(
        jnp.bfloat16
    )
    every_down, every_up = (
        lax.all_gather(rows_down, "dp", axis=0, tiled=True),
        lax.all_gather(rows_up, "dp", axis=0, tiled=True),
    )
    owned = group_index * per_owner + jnp.arange(per_owner, dtype=jnp.int32)
    mine = (every_slot[:, None] == owned[None, :]).astype(jnp.bfloat16)
    down_grad = jnp.einsum(
        "sp,srd->prd", mine, every_down, preferred_element_type=jnp.float32
    ).astype(jnp.bfloat16)
    up_grad = jnp.einsum("sp,srk->prk", mine, every_up, preferred_element_type=jnp.float32).astype(
        jnp.bfloat16
    )
    return (input_grad, down_grad, up_grad)


def device_program(layer_input, output_grad, key_weight, adapter_down, adapter_up, segment_adapter, adapter_slot, live_segments):
    args = (layer_input, output_grad, key_weight, adapter_down, adapter_up, segment_adapter, adapter_slot, live_segments)
    seg_group = segment_adapter.shape[0] // lax.axis_size("dp")
    one_each = seg_group == lax.axis_size("tensor")
    tiled = adapter_up.shape[2] % 128 == 0 and layer_input.shape[1] % 256 == 0
    if one_each and tiled and lax.axis_size("dp") % 2 == 0:
        return fused(*args)
    return on_device(*args)


def solution(mesh):
    in_specs = (
        P("dp", "tensor"),
        P(("dp", "tensor"), None),
        P("tensor", None),
        P("dp", None, "tensor"),
        P("dp", None, "tensor"),
        P(),
        P(),
        P("dp"),
    )
    out_specs = (P("dp", "tensor"), P("dp", None, "tensor"), P("dp", None, "tensor"))
    return jax.shard_map(
        device_program, mesh=mesh, in_specs=in_specs, out_specs=out_specs, check_vma=False
    )
```

```python
import functools

import jax
import jax.numpy as jnp
from jax import lax
from jax.experimental import pallas as pl
from jax.experimental.pallas import tpu as pltpu
from jax.sharding import PartitionSpec as P

MESH = pl.DeviceIdType.MESH
CHUNKS = 4
VMEM_LIMIT = 62 * 1024 * 1024
NT = (((1,), (1,)), ((), ()))
TN = (((0,), (0,)), ((), ()))


def fused_kernel(
    dims,
    adapter_hbm, slot_hbm, live_hbm,
    x_hbm, og_hbm, kw_hbm, ad_hbm, au_hbm,
    ig_hbm, dg_hbm, ug_hbm,
    adapter_s, slot_s, live_s, seg_slot, first,
    x_v, kw_v, ad_v, au_v, og_v, whole, ig_v, dg_v, ug_v,
    s1d_out, s1d_in, s2d_out, s2d_in, fu_out, fu_in,
    down_seg, up_seg, up_own, lr, pr_out, pr_in, su_out, su_in, rows_d, rows_u,
    load_sem, store_sem, blk_send, blk_recv, s1_send, s1_recv, s2_send, s2_recv, fu_send, fu_recv,
    up_send, up_recv, lr_send, lr_recv, pr_send, pr_recv, su_send, su_recv,
    rwy_send, rwu_send, rwc_send, rw_recv,
):
    T, X, Q, S, L, R, W, K, KS, PO = dims
    Z, Y = T // X, Q // 2
    half = L // CHUNKS
    t, q = lax.axis_index("tensor"), lax.axis_index("dp")
    z, x = t // X, lax.rem(t, X)
    y, c = q // 2, lax.rem(q, 2)
    mate = q + 1 - 2 * c
    pending = []

    def send(src, dst, send_sem, recv_sem, to, when=None):
        copy = pltpu.make_async_remote_copy(
            src_ref=src, dst_ref=dst, send_sem=send_sem, recv_sem=recv_sem,
            device_id=to, device_id_type=MESH,
        )
        if when is None:
            copy.start()
        else:
            pl.when(when)(copy.start)
        pending.append((when, copy))

    def arrived(ref, sem, when=None):
        copy = pltpu.make_async_copy(ref, ref, sem)
        if when is None:
            copy.wait()
        else:
            pl.when(when)(copy.wait)

    scalars = [
        pltpu.make_async_copy(adapter_hbm, adapter_s, load_sem.at[5]),
        pltpu.make_async_copy(slot_hbm, slot_s, load_sem.at[6]),
        pltpu.make_async_copy(live_hbm, live_s, load_sem.at[7]),
    ]
    loads = [
        pltpu.make_async_copy(og_hbm, og_v, load_sem.at[0]),
        pltpu.make_async_copy(au_hbm, au_v, load_sem.at[2]),
        pltpu.make_async_copy(ad_hbm, ad_v, load_sem.at[1]),
    ]
    later_loads = [
        pltpu.make_async_copy(x_hbm, x_v, load_sem.at[3]),
        pltpu.make_async_copy(kw_hbm, kw_v, load_sem.at[4]),
    ]
    for copy in scalars + loads:
        copy.start()

    tensor_peers = [lax.rem(t + j, T) for j in range(1, T)]
    far = [lax.rem(y + j, Y) for j in range(1, Y)]
    barrier = pltpu.get_barrier_semaphore()
    for peer in tensor_peers:
        pl.semaphore_signal(barrier, inc=1, device_id={"tensor": peer}, device_id_type=MESH)
    dp_peers = [lax.rem(q + j, Q) for j in range(1, Q)]
    for peer in dp_peers:
        pl.semaphore_signal(barrier, inc=1, device_id={"dp": peer}, device_id_type=MESH)

    scalars[2].wait()
    loads[0].wait()
    live = t < live_s[0]
    own_rows = jnp.where(live, og_v[...], jnp.zeros((L, K), jnp.bfloat16))
    whole[t] = own_rows
    pl.semaphore_wait(barrier, T - 1 + Q - 1)

    def rows_of(origin, part):
        return whole.at[origin, pl.ds(part * half, half)]

    def to_z(origin, part, up, when):
        step = 1 if up else -1
        edge = (z + 1 < Z) if up else (z > 0)
        when = edge if when is None else jnp.logical_and(when, edge)
        ref = rows_of(origin, part)
        send(ref, ref, blk_send.at[origin, part, 0 if up else 1], blk_recv.at[origin, part],
             {"tensor": t + step * X}, when)

    def to_x(origin, part, when):
        ref = rows_of(origin, part)
        for j in range(1, X):
            to = z * X + lax.rem(x + j, X)
            send(ref, ref, blk_send.at[origin, part, 1 + j], blk_recv.at[origin, part],
                 {"tensor": to}, when)

    direct = CHUNKS // 2
    pair_z = z + 1 - 2 * lax.rem(z, 2)
    column = z * X + lax.rem(x + 1, X)
    def start_own(part):
        to_z(t, part, True, None)
        to_z(t, part, False, None)
        to_x(t, part, None)

    start_own(0)
    start_own(1)

    def forward(step, part):
        for sign in (-1, 1):
            row = z + sign * step
            inside = jnp.logical_and(row >= 0, row < Z)
            origin = jnp.where(inside, row, z) * X + x
            arrived(rows_of(origin, part), blk_recv.at[origin, part], inside)
            to_z(origin, part, sign < 0, inside)
            across = inside
            if part >= direct:
                across = jnp.logical_and(inside, row != pair_z)
            to_x(origin, part, across)

    def share(part):
        ref = rows_of(column, part)
        send(ref, ref, blk_send.at[column, part, 0], blk_recv.at[column, part],
             {"tensor": pair_z * X + x})

    def combine_down(i, carry):
        group, s = i // S, lax.rem(i, S)
        inside, local = owned((group * 2 + c) * S + s)
        s2d_out[group, s] = jnp.where(inside, ad_v[local], s1d_in[group, s])
        return carry

    for copy in scalars[:2]:
        copy.wait()
    for s in range(Q * S):
        seg_slot[s] = slot_s[adapter_s[s]]

    def owned(index):
        local = seg_slot[index] - q * PO
        inside = jnp.logical_and(local >= 0, local < PO)
        return inside, jnp.clip(local, 0, PO - 1)

    loads[2].wait()

    def choose_down(i, carry):
        group, s = i // S, lax.rem(i, S)
        inside, local = owned((group * 2 + 1 - c) * S + s)
        s1d_out[group, s] = jnp.where(inside, ad_v[local], jnp.zeros((R, W), jnp.bfloat16))
        return carry

    lax.fori_loop(0, Y * S, choose_down, 0)
    loads[1].wait()

    def choose_up(i, carry):
        group, s = i // S, lax.rem(i, S)
        inside, local = owned(i)
        fu_out[group, s] = jnp.where(inside, au_v[local], jnp.zeros((R, KS), jnp.bfloat16))
        return carry

    lax.fori_loop(0, Q * S, choose_up, 0)
    for copy in later_loads:
        copy.start()
    send(s1d_out, s1d_in, s1_send.at[0], s1_recv.at[0], {"dp": mate})

    for peer in dp_peers:
        send(fu_out.at[peer], fu_in.at[q], fu_send.at[peer], fu_recv.at[q], {"dp": peer})
    start_own(2)
    start_own(3)

    def first_of(p, carry):
        slot = q * PO + p
        for group in range(Q):
            index = jnp.int32(-1)
            for s in reversed(range(S)):
                index = jnp.where(seg_slot[group * S + s] == slot, jnp.int32(s), index)
            first[p * Q + group] = index
        return carry

    lax.fori_loop(0, PO, first_of, 0)

    arrived(s1d_in, s1_recv.at[0])
    part_segs = S // 2

    def segs(piece):
        return pl.ds(piece * part_segs, part_segs)

    for piece in range(2):
        def combine_piece(i, carry):
            return combine_down(i // part_segs * S + piece * part_segs + lax.rem(i, part_segs), carry)

        lax.fori_loop(0, Y * part_segs, combine_piece, 0)
        for other in far:
            send(s2d_out.at[other, segs(piece)], s2d_in.at[y, segs(piece)], s2_send.at[other, piece],
                 s2_recv.at[y, piece], {"dp": other * 2 + c})
    total = fu_out[q]
    for peer in dp_peers:
        arrived(fu_in.at[peer], fu_recv.at[peer])
        total = total + fu_in[peer]
    up_seg[...] = total
    for peer in tensor_peers:
        send(up_seg.at[peer], up_own.at[t], up_send.at[peer], up_recv.at[t], {"tensor": peer})
    up_own[t] = up_seg[t]

    forward(1, 0)

    for peer in tensor_peers:
        arrived(up_own.at[peer], up_recv.at[peer])
    acc = jnp.zeros((R, L), jnp.float32)
    for p in range(T):
        acc = acc + lax.dot_general(
            up_own[p], whole[t, :, p * KS:(p + 1) * KS], NT, preferred_element_type=jnp.float32
        )
    lr[t] = acc.astype(jnp.bfloat16)
    for peer in tensor_peers:
        send(lr.at[t], lr.at[t], lr_send.at[peer], lr_recv.at[t], {"tensor": peer})

    forward(1, 1)
    forward(1, 2)

    later_loads[0].wait()

    def down_of(s, carry):
        rows = s2d_out[y, s]
        for other in far:
            rows = rows + s2d_in[other, s]
        down_seg[s] = rows
        pr_out[s] = lax.dot_general(rows, x_v[s], NT, preferred_element_type=jnp.float32)
        return carry

    def project(piece):
        for other in far:
            arrived(s2d_in.at[other, segs(piece)], s2_recv.at[other, piece])
        lax.fori_loop(piece * part_segs, (piece + 1) * part_segs, down_of, 0, unroll=2)
        for s in range(piece * part_segs, (piece + 1) * part_segs):
            remote = s != t
            send(pr_out.at[s], pr_in.at[t], pr_send.at[s], pr_recv.at[t], {"tensor": s}, remote)

            @pl.when(s == t)
            def _():
                pr_in[t] = pr_out[s]

    project(0)
    forward(1, 3)

    for peer in tensor_peers:
        arrived(lr.at[peer], lr_recv.at[peer])

    own_slots = [seg_slot[q * S + s] for s in range(S)]

    def merged(parts, u, zero):
        return [jnp.where(own_slots[u] == own_slots[s], parts[s], zero) for s in range(S)]

    zero_l = jnp.zeros((R, L), jnp.bfloat16)
    ranks = [lr[s] for s in range(S)]
    left = jnp.concatenate(
        [jnp.concatenate(merged(ranks, u, zero_l), axis=1) for u in range(S)], axis=0
    )
    tile = 256
    for n in range(W // tile):
        columns = slice(n * tile, (n + 1) * tile)
        right = jnp.concatenate([x_v[s, :, columns] for s in range(S)], axis=0)
        grad = 2.0 * jnp.dot(left, right, preferred_element_type=jnp.float32)
        rows_d[q, :, :, columns] = grad.astype(jnp.bfloat16).reshape(S, R, tile)
    for other in far:
        send(rows_d.at[q], rows_d.at[q], rwy_send.at[other], rw_recv.at[q, 0],
             {"dp": other * 2 + c})
    send(rows_d.at[q], rows_d.at[q], rwc_send.at[q], rw_recv.at[q, 0], {"dp": mate})

    forward(2, 0)
    project(1)
    forward(2, 1)
    later_loads[1].wait()

    def two_blocks(pair):
        left_rows = jnp.concatenate([whole[origin] for origin in pair], axis=0)
        for n in range(W // tile):
            at = slice(n * tile, (n + 1) * tile)
            value = lax.dot_general(left_rows, kw_v[at, :], NT, preferred_element_type=jnp.float32)
            for j, origin in enumerate(pair):
                extra = lax.dot_general(
                    lr[origin], down_seg[origin, :, at], TN, preferred_element_type=jnp.float32
                )
                ig_v[origin, :, at] = (value[j * L:(j + 1) * L] + 2.0 * extra).astype(jnp.bfloat16)
        for origin in pair:
            pltpu.make_async_copy(ig_v.at[origin], ig_hbm.at[origin], store_sem.at[origin]).start()

    def wait_side(origin, parts):
        for part in parts:
            arrived(rows_of(origin, part), blk_recv.at[origin, part])

    lower = z < 2
    near_row, far_row = jnp.where(lower, 2, 1), jnp.where(lower, 3, 0)
    other = lax.rem(x + 1, X)

    wait_side(column, range(CHUNKS))
    two_blocks((t, column))
    forward(2, 2)

    for peer in tensor_peers:
        arrived(pr_in.at[peer], pr_recv.at[peer])
    acc = pr_in[0]
    for p in range(1, T):
        acc = acc + pr_in[p]
    projected = acc.astype(jnp.bfloat16)
    for p in range(T):
        su_out[p] = 2.0 * jnp.dot(
            projected, whole[t, :, p * KS:(p + 1) * KS], preferred_element_type=jnp.float32
        )
    for peer in tensor_peers:
        send(su_out.at[peer], su_in.at[t], su_send.at[peer], su_recv.at[t], {"tensor": peer})
    su_in[t] = su_out[t]

    forward(2, 3)
    for part in range(direct, CHUNKS):
        share(part)
    forward(3, 0)
    two_blocks((pair_z * X + x, near_row * X + x))
    forward(3, 1)

    for peer in tensor_peers:
        arrived(su_in.at[peer], su_recv.at[peer])
    zero_u = jnp.zeros((R, KS), jnp.float32)
    for u in range(S):
        total = zero_u
        for s in range(S):
            total = total + jnp.where(own_slots[u] == own_slots[s], su_in[s], zero_u)
        rows_u[q, u] = total.astype(jnp.bfloat16)
    for peer in dp_peers:
        send(rows_u.at[q], rows_u.at[q], rwu_send.at[peer], rw_recv.at[q, 1], {"dp": peer})

    forward(3, 2)
    for far_chip in far:
        origin = far_chip * 2 + c
        arrived(rows_d.at[origin], rw_recv.at[origin, 0])
        send(rows_d.at[origin], rows_d.at[origin], rwc_send.at[origin],
             rw_recv.at[origin, 0], {"dp": mate})
    forward(3, 3)
    wait_side(near_row * X + other, range(CHUNKS))
    two_blocks((far_row * X + x, near_row * X + other))

    for group in range(Y):
        origin = group * 2 + 1 - c
        arrived(rows_d.at[origin], rw_recv.at[origin, 0])

    def owner_sum(rows, out, p, width):
        total = jnp.zeros((R, width), jnp.float32)
        for group in range(Q):
            index = first[p * Q + group]
            row = rows[group, jnp.maximum(index, 0)].astype(jnp.float32)
            total += jnp.where(index >= 0, row, 0.0)
        out[p] = total.astype(jnp.bfloat16)

    def owner_down(p, carry):
        owner_sum(rows_d, dg_v, p, W)
        return carry

    def owner_up(p, carry):
        owner_sum(rows_u, ug_v, p, KS)
        return carry

    lax.fori_loop(0, PO, owner_down, 0, unroll=2)
    stores = [
        pltpu.make_async_copy(dg_v, dg_hbm, store_sem.at[T]),
        pltpu.make_async_copy(ug_v, ug_hbm, store_sem.at[T + 1]),
    ]
    stores[0].start()

    wait_side(far_row * X + other, range(CHUNKS))
    wait_side(pair_z * X + other, range(CHUNKS))
    two_blocks((pair_z * X + other, far_row * X + other))

    for peer in dp_peers:
        arrived(rows_u.at[peer], rw_recv.at[peer, 1])
    lax.fori_loop(0, PO, owner_up, 0, unroll=4)
    stores[1].start()

    for when, copy in pending:
        if when is None:
            copy.wait_send()
        else:
            pl.when(when)(copy.wait_send)
    for origin in range(T):
        pltpu.make_async_copy(ig_v.at[origin], ig_hbm.at[origin], store_sem.at[origin]).wait()
    for copy in stores:
        copy.wait()


def store_kernel(a, b, c, a_out, b_out, c_out, a_v, b_v, c_v, in_sem, out_sem):
    moves = []
    for src, held, dst, pieces in ((a, a_v, a_out, 4), (b, b_v, b_out, 2), (c, c_v, c_out, 1)):
        count = src.shape[0] // pieces
        for i in range(pieces):
            at, n = pl.ds(i * count, count), len(moves)
            moves.append((
                pltpu.make_async_copy(src.at[at], held.at[at], in_sem.at[n]),
                pltpu.make_async_copy(held.at[at], dst.at[at], out_sem.at[n]),
            ))
    for load, _ in moves:
        load.start()
    for load, store in moves:
        load.wait()
        store.start()
    for _, store in moves:
        store.wait()


def fused(layer_input, output_grad, key_weight, adapter_down, adapter_up, segment_adapter, adapter_slot, live_segments):
    T, Q = lax.axis_size("tensor"), lax.axis_size("dp")
    X = 1 << ((T.bit_length() - 1) // 2)
    W = layer_input.shape[1]
    L, K = output_grad.shape
    PO, R, KS = adapter_up.shape
    S = segment_adapter.shape[0] // Q
    Y = Q // 2
    dims = (T, X, Q, S, L, R, W, K, KS, PO)
    bf, f32 = jnp.bfloat16, jnp.float32
    V, DMA = pltpu.VMEM, pltpu.SemaphoreType.DMA
    far_in = pl.BlockSpec(memory_space=pltpu.HBM)
    hbm = pl.BlockSpec(memory_space=pl.ANY)
    flops = 2 * T * L * K * W + 8 * T * L * R * W
    input_grad, down_grad, up_grad = pl.pallas_call(
        functools.partial(fused_kernel, dims),
        out_shape=(
            jax.ShapeDtypeStruct((T, L, W), bf),
            jax.ShapeDtypeStruct((PO, R, W), bf),
            jax.ShapeDtypeStruct((PO, R, KS), bf),
        ),
        in_specs=[far_in] * 8,
        out_specs=(hbm,) * 3,
        scratch_shapes=[
            pltpu.SMEM((Q * S,), jnp.int32), pltpu.SMEM((adapter_slot.shape[0],), jnp.int32),
            pltpu.SMEM((1,), jnp.int32), pltpu.SMEM((Q * S,), jnp.int32),
            pltpu.SMEM((PO * Q,), jnp.int32),
            V((T, L, W), bf), V((W, K), bf), V((PO, R, W), bf), V((PO, R, KS), bf), V((L, K), bf),
            V((T, L, K), bf), V((T, L, W), bf), V((PO, R, W), bf), V((PO, R, KS), bf),
            V((Y, S, R, W), bf), V((Y, S, R, W), bf), V((Y, S, R, W), bf), V((Y, S, R, W), bf),
            V((Q, S, R, KS), bf), V((Q, S, R, KS), bf),
            V((S, R, W), bf), V((S, R, KS), bf), V((T, R, KS), bf), V((T, R, L), bf),
            V((S, R, L), f32), V((T, R, L), f32), V((T, R, KS), f32), V((T, R, KS), f32),
            V((Q, S, R, W), bf), V((Q, S, R, KS), bf),
            DMA((8,)), DMA((T + 2,)), DMA((T, CHUNKS, 1 + X)), DMA((T, CHUNKS)),
            DMA((2,)), DMA((2,)), DMA((Y, 2)), DMA((Y, 2)), DMA((Q,)), DMA((Q,)),
            DMA((T,)), DMA((T,)), DMA((T,)), DMA((T,)),
            DMA((T,)), DMA((T,)), DMA((T,)), DMA((T,)),
            DMA((Y,)), DMA((Q,)), DMA((Q,)), DMA((Q, 2)),
        ],
        compiler_params=pltpu.CompilerParams(
            collective_id=0, has_side_effects=True, vmem_limit_bytes=VMEM_LIMIT
        ),
        cost_estimate=pl.CostEstimate(
            flops=flops, bytes_accessed=2 * (2 * T * L * W + K * W + 2 * PO * R * W), transcendentals=0
        ),
    )(
        segment_adapter, adapter_slot, live_segments,
        layer_input.reshape(T, L, W), output_grad, key_weight, adapter_down, adapter_up,
    )
    results = (input_grad, down_grad, up_grad)
    input_grad, down_grad, up_grad = pl.pallas_call(
        store_kernel,
        out_shape=tuple(jax.ShapeDtypeStruct(r.shape, r.dtype) for r in results),
        in_specs=[hbm] * 3,
        out_specs=(hbm,) * 3,
        scratch_shapes=[V(r.shape, r.dtype) for r in results] + [DMA((7,)), DMA((7,))],
        compiler_params=pltpu.CompilerParams(vmem_limit_bytes=VMEM_LIMIT),
        cost_estimate=pl.CostEstimate(
            flops=0, bytes_accessed=4 * (T * L * W + PO * R * W), transcendentals=0
        ),
    )(*results)
    return input_grad.reshape(T * L, W), down_grad, up_grad


def on_device(
    layer_input,
    output_grad,
    key_weight,
    adapter_down,
    adapter_up,
    segment_adapter,
    adapter_slot,
    live_segments,
):
    tensor_size = lax.axis_size("tensor")
    position = lax.axis_index("tensor")
    group_count = lax.axis_size("dp")
    group_index = lax.axis_index("dp")
    row_count = output_grad.shape[0]
    tok_group = layer_input.shape[0]
    width_shard = layer_input.shape[1]
    key_width = output_grad.shape[1]
    key_shard = key_width // tensor_size
    adapters = adapter_slot.shape[0]
    rank_dim = adapter_down.shape[1]
    seg_total = segment_adapter.shape[0]
    seg_group = seg_total // group_count
    seg_len = tok_group // seg_group
    per_owner = adapters // group_count
    slot_ids = jnp.arange(adapters, dtype=jnp.int32)
    lookup = segment_adapter[:, None] == slot_ids[None, :]
    every_slot = jnp.sum(jnp.where(lookup, adapter_slot[None, :], 0), axis=1)
    seg_slot = lax.dynamic_slice_in_dim(every_slot, group_index * seg_group, seg_group)
    local_rows = position * row_count + jnp.arange(row_count, dtype=jnp.int32)
    live_rows = local_rows // seg_len < live_segments[0]
    masked = jnp.where(live_rows[:, None], output_grad, jnp.zeros_like(output_grad))
    whole = lax.all_gather(masked, "tensor", axis=0, tiled=True)
    stores = (
        lax.all_gather(adapter_down, "dp", axis=0, tiled=True),
        lax.all_gather(adapter_up, "dp", axis=0, tiled=True),
    )
    choose = (seg_slot[:, None] == slot_ids[None, :]).astype(jnp.bfloat16)
    down_seg = jnp.dot(choose, stores[0].reshape(adapters, -1), preferred_element_type=jnp.float32)
    down_seg = down_seg.astype(jnp.bfloat16).reshape(seg_group, rank_dim, width_shard)
    up_seg = jnp.dot(choose, stores[1].reshape(adapters, -1), preferred_element_type=jnp.float32)
    up_seg = up_seg.astype(jnp.bfloat16).reshape(seg_group, rank_dim, key_shard)
    own_keys = lax.dynamic_slice_in_dim(whole, position * key_shard, key_shard, 1).reshape(
        seg_group, seg_len, key_shard
    )
    input_seg = layer_input.reshape(seg_group, seg_len, width_shard)
    up_part = jnp.einsum("sjk,srk->rsj", own_keys, up_seg, preferred_element_type=jnp.float32)
    down_part = jnp.einsum("sjd,srd->rsj", input_seg, down_seg, preferred_element_type=jnp.float32)
    lowrank, projected = lax.psum((up_part, down_part), "tensor")
    lowrank = lowrank.astype(jnp.bfloat16)
    projected = projected.astype(jnp.bfloat16)
    frozen = lax.dot_general(
        whole, key_weight, (((1,), (1,)), ((), ())), preferred_element_type=jnp.float32
    )
    extra = jnp.einsum("rsj,srd->sjd", lowrank, down_seg, preferred_element_type=jnp.float32)
    input_grad = (frozen + 2.0 * extra.reshape(tok_group, width_shard)).astype(jnp.bfloat16)
    seg_down = 2.0 * jnp.einsum(
        "rsj,sjd->srd", lowrank, input_seg, preferred_element_type=jnp.float32
    )
    seg_up = 2.0 * jnp.einsum(
        "rsj,sjk->srk", projected, own_keys, preferred_element_type=jnp.float32
    )
    seg_index = jnp.arange(seg_group, dtype=jnp.int32)
    same = seg_slot[:, None] == seg_slot[None, :]
    earlier = same & (seg_index[None, :] < seg_index[:, None])
    leading = jnp.logical_not(jnp.any(earlier, axis=1))
    merge_rows = (same & leading[:, None]).astype(jnp.float32)
    rows_down = jnp.einsum(
        "us,srd->urd", merge_rows, seg_down, precision=lax.Precision.HIGHEST
    ).astype(jnp.bfloat16)
    rows_up = jnp.einsum("us,srk->urk", merge_rows, seg_up, precision=lax.Precision.HIGHEST).astype(
        jnp.bfloat16
    )
    every_down, every_up = (
        lax.all_gather(rows_down, "dp", axis=0, tiled=True),
        lax.all_gather(rows_up, "dp", axis=0, tiled=True),
    )
    owned = group_index * per_owner + jnp.arange(per_owner, dtype=jnp.int32)
    mine = (every_slot[:, None] == owned[None, :]).astype(jnp.bfloat16)
    down_grad = jnp.einsum(
        "sp,srd->prd", mine, every_down, preferred_element_type=jnp.float32
    ).astype(jnp.bfloat16)
    up_grad = jnp.einsum("sp,srk->prk", mine, every_up, preferred_element_type=jnp.float32).astype(
        jnp.bfloat16
    )
    return (input_grad, down_grad, up_grad)


def device_program(layer_input, output_grad, key_weight, adapter_down, adapter_up, segment_adapter, adapter_slot, live_segments):
    args = (layer_input, output_grad, key_weight, adapter_down, adapter_up, segment_adapter, adapter_slot, live_segments)
    seg_group = segment_adapter.shape[0] // lax.axis_size("dp")
    one_each = seg_group == lax.axis_size("tensor") == 8
    tiled = adapter_up.shape[2] % 128 == 0 and layer_input.shape[1] % 256 == 0
    if one_each and tiled and lax.axis_size("dp") % 2 == 0:
        return fused(*args)
    return on_device(*args)


def solution(mesh):
    in_specs = (
        P("dp", "tensor"),
        P(("dp", "tensor"), None),
        P("tensor", None),
        P("dp", None, "tensor"),
        P("dp", None, "tensor"),
        P(),
        P(),
        P("dp"),
    )
    out_specs = (P("dp", "tensor"), P("dp", None, "tensor"), P("dp", None, "tensor"))
    return jax.shard_map(
        device_program, mesh=mesh, in_specs=in_specs, out_specs=out_specs, check_vma=False
    )
```

```python
import functools

import jax
import jax.numpy as jnp
from jax import lax
from jax.experimental import pallas as pl
from jax.experimental.pallas import tpu as pltpu
from jax.sharding import PartitionSpec as P

MESH = pl.DeviceIdType.MESH
CHUNKS = 4
VMEM_LIMIT = 62 * 1024 * 1024
NT = (((1,), (1,)), ((), ()))
TN = (((0,), (0,)), ((), ()))


def fused_kernel(
    dims,
    adapter_hbm, slot_hbm, live_hbm,
    x_hbm, og_hbm, kw_hbm, ad_hbm, au_hbm,
    ig_hbm, dg_hbm, ug_hbm,
    adapter_s, slot_s, live_s, seg_slot, first,
    x_v, kw_v, ad_v, au_v, og_v, whole, ig_v, dg_v, ug_v,
    s1d_out, s1d_in, s2d_out, s2d_in, fu_out, fu_in,
    down_seg, up_seg, up_own, lr, pr_out, pr_in, su_out, su_in, rows_d, rows_u,
    load_sem, store_sem, blk_send, blk_recv, s1_send, s1_recv, s2_send, s2_recv, fu_send, fu_recv,
    up_send, up_recv, lr_send, lr_recv, pr_send, pr_recv, su_send, su_recv,
    rwy_send, rwu_send, rwc_send, rw_recv,
):
    T, X, Q, S, L, R, W, K, KS, PO = dims
    Z, Y = T // X, Q // 2
    half = L // CHUNKS
    t, q = lax.axis_index("tensor"), lax.axis_index("dp")
    z, x = t // X, lax.rem(t, X)
    y, c = q // 2, lax.rem(q, 2)
    mate = q + 1 - 2 * c
    pending = []

    def send(src, dst, send_sem, recv_sem, to, when=None):
        copy = pltpu.make_async_remote_copy(
            src_ref=src, dst_ref=dst, send_sem=send_sem, recv_sem=recv_sem,
            device_id=to, device_id_type=MESH,
        )
        if when is None:
            copy.start()
        else:
            pl.when(when)(copy.start)
        pending.append((when, copy))

    def arrived(ref, sem, when=None):
        copy = pltpu.make_async_copy(ref, ref, sem)
        if when is None:
            copy.wait()
        else:
            pl.when(when)(copy.wait)

    scalars = [
        pltpu.make_async_copy(adapter_hbm, adapter_s, load_sem.at[5]),
        pltpu.make_async_copy(slot_hbm, slot_s, load_sem.at[6]),
        pltpu.make_async_copy(live_hbm, live_s, load_sem.at[7]),
    ]
    loads = [
        pltpu.make_async_copy(og_hbm, og_v, load_sem.at[0]),
        pltpu.make_async_copy(au_hbm, au_v, load_sem.at[2]),
        pltpu.make_async_copy(ad_hbm, ad_v, load_sem.at[1]),
    ]
    later_loads = [
        pltpu.make_async_copy(x_hbm, x_v, load_sem.at[3]),
        pltpu.make_async_copy(kw_hbm, kw_v, load_sem.at[4]),
    ]
    tensor_peers = [lax.rem(t + j, T) for j in range(1, T)]
    far = [lax.rem(y + j, Y) for j in range(1, Y)]
    barrier = pltpu.get_barrier_semaphore()
    for peer in tensor_peers:
        pl.semaphore_signal(barrier, inc=1, device_id={"tensor": peer}, device_id_type=MESH)
    dp_peers = [lax.rem(q + j, Q) for j in range(1, Q)]
    for peer in dp_peers:
        pl.semaphore_signal(barrier, inc=1, device_id={"dp": peer}, device_id_type=MESH)

    for copy in scalars[2:] + loads[:1] + scalars[:2] + loads[1:]:
        copy.start()

    scalars[2].wait()
    loads[0].wait()
    live = t < live_s[0]
    own_rows = jnp.where(live, og_v[...], jnp.zeros((L, K), jnp.bfloat16))
    whole[t] = own_rows
    pl.semaphore_wait(barrier, T - 1 + Q - 1)

    def rows_of(origin, part):
        return whole.at[origin, pl.ds(part * half, half)]

    def to_z(origin, part, up, when):
        step = 1 if up else -1
        edge = (z + 1 < Z) if up else (z > 0)
        when = edge if when is None else jnp.logical_and(when, edge)
        ref = rows_of(origin, part)
        send(ref, ref, blk_send.at[origin, part, 0 if up else 1], blk_recv.at[origin, part],
             {"tensor": t + step * X}, when)

    def to_x(origin, part, when):
        ref = rows_of(origin, part)
        for j in range(1, X):
            to = z * X + lax.rem(x + j, X)
            send(ref, ref, blk_send.at[origin, part, 1 + j], blk_recv.at[origin, part],
                 {"tensor": to}, when)

    direct = CHUNKS // 2
    pair_z = z + 1 - 2 * lax.rem(z, 2)
    column = z * X + lax.rem(x + 1, X)
    def start_own(part):
        to_z(t, part, True, None)
        to_z(t, part, False, None)
        to_x(t, part, None)

    start_own(0)
    start_own(1)

    def forward(step, part):
        for sign in (-1, 1):
            row = z + sign * step
            inside = jnp.logical_and(row >= 0, row < Z)
            origin = jnp.where(inside, row, z) * X + x
            arrived(rows_of(origin, part), blk_recv.at[origin, part], inside)
            to_z(origin, part, sign < 0, inside)
            across = inside
            if part >= direct:
                across = jnp.logical_and(inside, row != pair_z)
            to_x(origin, part, across)

    def share(part):
        ref = rows_of(column, part)
        send(ref, ref, blk_send.at[column, part, 0], blk_recv.at[column, part],
             {"tensor": pair_z * X + x})

    def combine_down(i, carry):
        group, s = i // S, lax.rem(i, S)
        inside, local = owned((group * 2 + c) * S + s)
        s2d_out[group, s] = jnp.where(inside, ad_v[local], s1d_in[group, s])
        return carry

    for copy in scalars[:2]:
        copy.wait()
    for s in range(Q * S):
        seg_slot[s] = slot_s[adapter_s[s]]

    def owned(index):
        local = seg_slot[index] - q * PO
        inside = jnp.logical_and(local >= 0, local < PO)
        return inside, jnp.clip(local, 0, PO - 1)

    loads[2].wait()

    def choose_down(i, carry):
        group, s = i // S, lax.rem(i, S)
        inside, local = owned((group * 2 + 1 - c) * S + s)
        s1d_out[group, s] = jnp.where(inside, ad_v[local], jnp.zeros((R, W), jnp.bfloat16))
        return carry

    lax.fori_loop(0, Y * S, choose_down, 0)
    send(s1d_out, s1d_in, s1_send.at[0], s1_recv.at[0], {"dp": mate})

    loads[1].wait()

    def choose_up(i, carry):
        group, s = i // S, lax.rem(i, S)
        inside, local = owned(i)
        fu_out[group, s] = jnp.where(inside, au_v[local], jnp.zeros((R, KS), jnp.bfloat16))
        return carry

    lax.fori_loop(0, Q * S, choose_up, 0)
    for copy in later_loads:
        copy.start()
    for peer in dp_peers:
        send(fu_out.at[peer], fu_in.at[q], fu_send.at[peer], fu_recv.at[q], {"dp": peer})
    start_own(2)
    start_own(3)

    forward(1, 0)

    total = fu_out[q]
    for peer in dp_peers:
        arrived(fu_in.at[peer], fu_recv.at[peer])
        total = total + fu_in[peer]
    up_seg[...] = total
    for peer in tensor_peers:
        send(up_seg.at[peer], up_own.at[t], up_send.at[peer], up_recv.at[t], {"tensor": peer})
    up_own[t] = up_seg[t]

    arrived(s1d_in, s1_recv.at[0])
    part_segs = S // 2

    def segs(piece):
        return pl.ds(piece * part_segs, part_segs)

    for piece in range(2):
        def combine_piece(i, carry):
            return combine_down(i // part_segs * S + piece * part_segs + lax.rem(i, part_segs), carry)

        lax.fori_loop(0, Y * part_segs, combine_piece, 0)
        for other in far:
            send(s2d_out.at[other, segs(piece)], s2d_in.at[y, segs(piece)], s2_send.at[other, piece],
                 s2_recv.at[y, piece], {"dp": other * 2 + c})

    forward(1, 1)
    forward(1, 2)

    for peer in tensor_peers:
        arrived(up_own.at[peer], up_recv.at[peer])
    acc = jnp.zeros((R, L), jnp.float32)
    for p in range(T):
        acc = acc + lax.dot_general(
            up_own[p], whole[t, :, p * KS:(p + 1) * KS], NT, preferred_element_type=jnp.float32
        )
    lr[t] = acc.astype(jnp.bfloat16)
    for peer in tensor_peers:
        send(lr.at[t], lr.at[t], lr_send.at[peer], lr_recv.at[t], {"tensor": peer})

    forward(1, 3)
    forward(2, 0)


    def down_of(s, carry):
        rows = s2d_out[y, s]
        for other in far:
            rows = rows + s2d_in[other, s]
        down_seg[s] = rows
        pr_out[s] = lax.dot_general(rows, x_v[s], NT, preferred_element_type=jnp.float32)
        return carry

    def project(piece):
        for other in far:
            arrived(s2d_in.at[other, segs(piece)], s2_recv.at[other, piece])
        lax.fori_loop(piece * part_segs, (piece + 1) * part_segs, down_of, 0, unroll=2)
        for s in range(piece * part_segs, (piece + 1) * part_segs):
            remote = s != t
            send(pr_out.at[s], pr_in.at[t], pr_send.at[s], pr_recv.at[t], {"tensor": s}, remote)

            @pl.when(s == t)
            def _():
                pr_in[t] = pr_out[s]

    later_loads[0].wait()

    for peer in tensor_peers:
        arrived(lr.at[peer], lr_recv.at[peer])

    own_slots = [seg_slot[q * S + s] for s in range(S)]

    def merged(parts, u, zero):
        return [jnp.where(own_slots[u] == own_slots[s], parts[s], zero) for s in range(S)]

    zero_l = jnp.zeros((R, L), jnp.bfloat16)
    ranks = [lr[s] for s in range(S)]
    left = jnp.concatenate(
        [jnp.concatenate(merged(ranks, u, zero_l), axis=1) for u in range(S)], axis=0
    )
    tile = 256
    for n in range(W // tile):
        columns = slice(n * tile, (n + 1) * tile)
        right = jnp.concatenate([x_v[s, :, columns] for s in range(S)], axis=0)
        grad = 2.0 * jnp.dot(left, right, preferred_element_type=jnp.float32)
        rows_d[q, :, :, columns] = grad.astype(jnp.bfloat16).reshape(S, R, tile)
    for other in far:
        send(rows_d.at[q], rows_d.at[q], rwy_send.at[other], rw_recv.at[q, 0],
             {"dp": other * 2 + c})
    send(rows_d.at[q], rows_d.at[q], rwc_send.at[q], rw_recv.at[q, 0], {"dp": mate})

    forward(2, 1)
    project(0)
    forward(2, 2)
    project(1)
    forward(2, 3)


    def two_blocks(pair):
        left_rows = jnp.concatenate([whole[origin] for origin in pair], axis=0)
        for n in range(W // tile):
            at = slice(n * tile, (n + 1) * tile)
            value = lax.dot_general(left_rows, kw_v[at, :], NT, preferred_element_type=jnp.float32)
            for j, origin in enumerate(pair):
                extra = lax.dot_general(
                    lr[origin], down_seg[origin, :, at], TN, preferred_element_type=jnp.float32
                )
                ig_v[origin, :, at] = (value[j * L:(j + 1) * L] + 2.0 * extra).astype(jnp.bfloat16)
        for origin in pair:
            pltpu.make_async_copy(ig_v.at[origin], ig_hbm.at[origin], store_sem.at[origin]).start()

    def wait_side(origin, parts):
        for part in parts:
            arrived(rows_of(origin, part), blk_recv.at[origin, part])

    lower = z < 2
    near_row, far_row = jnp.where(lower, 2, 1), jnp.where(lower, 3, 0)
    other = lax.rem(x + 1, X)

    wait_side(column, range(CHUNKS))
    for part in range(direct, CHUNKS):
        share(part)
    forward(3, 0)
    later_loads[1].wait()
    two_blocks((t, column))

    for peer in tensor_peers:
        arrived(pr_in.at[peer], pr_recv.at[peer])
    acc = pr_in[0]
    for p in range(1, T):
        acc = acc + pr_in[p]
    projected = acc.astype(jnp.bfloat16)
    for p in range(T):
        su_out[p] = 2.0 * jnp.dot(
            projected, whole[t, :, p * KS:(p + 1) * KS], preferred_element_type=jnp.float32
        )
    for peer in tensor_peers:
        send(su_out.at[peer], su_in.at[t], su_send.at[peer], su_recv.at[t], {"tensor": peer})
    su_in[t] = su_out[t]

    forward(3, 1)

    def first_of(p, carry):
        slot = q * PO + p
        for group in range(Q):
            index = jnp.int32(-1)
            for s in reversed(range(S)):
                index = jnp.where(seg_slot[group * S + s] == slot, jnp.int32(s), index)
            first[p * Q + group] = index
        return carry

    lax.fori_loop(0, PO, first_of, 0)

    for peer in tensor_peers:
        arrived(su_in.at[peer], su_recv.at[peer])
    zero_u = jnp.zeros((R, KS), jnp.float32)
    for u in range(S):
        total = zero_u
        for s in range(S):
            total = total + jnp.where(own_slots[u] == own_slots[s], su_in[s], zero_u)
        rows_u[q, u] = total.astype(jnp.bfloat16)
    for peer in dp_peers:
        send(rows_u.at[q], rows_u.at[q], rwu_send.at[peer], rw_recv.at[q, 1], {"dp": peer})

    settled = list(pending)
    pending.clear()
    forward(3, 2)
    forward(3, 3)
    two_blocks((pair_z * X + x, near_row * X + x))

    for far_chip in far:
        origin = far_chip * 2 + c
        arrived(rows_d.at[origin], rw_recv.at[origin, 0])
        send(rows_d.at[origin], rows_d.at[origin], rwc_send.at[origin],
             rw_recv.at[origin, 0], {"dp": mate})
    wait_side(near_row * X + other, range(CHUNKS))
    two_blocks((far_row * X + x, near_row * X + other))

    for group in range(Y):
        origin = group * 2 + 1 - c
        arrived(rows_d.at[origin], rw_recv.at[origin, 0])

    def owner_sum(rows, out, p, width):
        total = jnp.zeros((R, width), jnp.float32)
        for group in range(Q):
            index = first[p * Q + group]
            row = rows[group, jnp.maximum(index, 0)].astype(jnp.float32)
            total += jnp.where(index >= 0, row, 0.0)
        out[p] = total.astype(jnp.bfloat16)

    def owner_down(p, carry):
        owner_sum(rows_d, dg_v, p, W)
        return carry

    def owner_up(p, carry):
        owner_sum(rows_u, ug_v, p, KS)
        return carry

    lax.fori_loop(0, PO, owner_down, 0, unroll=2)
    stores = [
        pltpu.make_async_copy(dg_v, dg_hbm, store_sem.at[T]),
        pltpu.make_async_copy(ug_v, ug_hbm, store_sem.at[T + 1]),
    ]
    stores[0].start()

    for peer in dp_peers:
        arrived(rows_u.at[peer], rw_recv.at[peer, 1])
    lax.fori_loop(0, PO, owner_up, 0, unroll=4)
    stores[1].start()

    def settle(sends):
        for when, copy in sends:
            if when is None:
                copy.wait_send()
            else:
                pl.when(when)(copy.wait_send)

    settle(settled)
    wait_side(far_row * X + other, range(CHUNKS))
    wait_side(pair_z * X + other, range(CHUNKS))
    two_blocks((pair_z * X + other, far_row * X + other))

    settle(pending)
    for origin in range(T):
        pltpu.make_async_copy(ig_v.at[origin], ig_hbm.at[origin], store_sem.at[origin]).wait()
    for copy in stores:
        copy.wait()


def store_kernel(a, b, c, a_out, b_out, c_out, a_v, b_v, c_v, in_sem, out_sem):
    moves = []
    for src, held, dst, pieces in ((a, a_v, a_out, 4), (b, b_v, b_out, 2), (c, c_v, c_out, 1)):
        count = src.shape[0] // pieces
        for i in range(pieces):
            at, n = pl.ds(i * count, count), len(moves)
            moves.append((
                pltpu.make_async_copy(src.at[at], held.at[at], in_sem.at[n]),
                pltpu.make_async_copy(held.at[at], dst.at[at], out_sem.at[n]),
            ))
    for load, _ in moves:
        load.start()
    for load, store in moves:
        load.wait()
        store.start()
    for _, store in moves:
        store.wait()


def fused(layer_input, output_grad, key_weight, adapter_down, adapter_up, segment_adapter, adapter_slot, live_segments):
    T, Q = lax.axis_size("tensor"), lax.axis_size("dp")
    X = 1 << ((T.bit_length() - 1) // 2)
    W = layer_input.shape[1]
    L, K = output_grad.shape
    PO, R, KS = adapter_up.shape
    S = segment_adapter.shape[0] // Q
    Y = Q // 2
    dims = (T, X, Q, S, L, R, W, K, KS, PO)
    bf, f32 = jnp.bfloat16, jnp.float32
    V, DMA = pltpu.VMEM, pltpu.SemaphoreType.DMA
    far_in = pl.BlockSpec(memory_space=pltpu.HBM)
    hbm = pl.BlockSpec(memory_space=pl.ANY)
    flops = 2 * T * L * K * W + 8 * T * L * R * W
    input_grad, down_grad, up_grad = pl.pallas_call(
        functools.partial(fused_kernel, dims),
        out_shape=(
            jax.ShapeDtypeStruct((T, L, W), bf),
            jax.ShapeDtypeStruct((PO, R, W), bf),
            jax.ShapeDtypeStruct((PO, R, KS), bf),
        ),
        in_specs=[far_in] * 8,
        out_specs=(hbm,) * 3,
        scratch_shapes=[
            pltpu.SMEM((Q * S,), jnp.int32), pltpu.SMEM((adapter_slot.shape[0],), jnp.int32),
            pltpu.SMEM((1,), jnp.int32), pltpu.SMEM((Q * S,), jnp.int32),
            pltpu.SMEM((PO * Q,), jnp.int32),
            V((T, L, W), bf), V((W, K), bf), V((PO, R, W), bf), V((PO, R, KS), bf), V((L, K), bf),
            V((T, L, K), bf), V((T, L, W), bf), V((PO, R, W), bf), V((PO, R, KS), bf),
            V((Y, S, R, W), bf), V((Y, S, R, W), bf), V((Y, S, R, W), bf), V((Y, S, R, W), bf),
            V((Q, S, R, KS), bf), V((Q, S, R, KS), bf),
            V((S, R, W), bf), V((S, R, KS), bf), V((T, R, KS), bf), V((T, R, L), bf),
            V((S, R, L), f32), V((T, R, L), f32), V((T, R, KS), f32), V((T, R, KS), f32),
            V((Q, S, R, W), bf), V((Q, S, R, KS), bf),
            DMA((8,)), DMA((T + 2,)), DMA((T, CHUNKS, 1 + X)), DMA((T, CHUNKS)),
            DMA((2,)), DMA((2,)), DMA((Y, 2)), DMA((Y, 2)), DMA((Q,)), DMA((Q,)),
            DMA((T,)), DMA((T,)), DMA((T,)), DMA((T,)),
            DMA((T,)), DMA((T,)), DMA((T,)), DMA((T,)),
            DMA((Y,)), DMA((Q,)), DMA((Q,)), DMA((Q, 2)),
        ],
        compiler_params=pltpu.CompilerParams(
            collective_id=0, has_side_effects=True, vmem_limit_bytes=VMEM_LIMIT
        ),
        cost_estimate=pl.CostEstimate(
            flops=flops, bytes_accessed=2 * (2 * T * L * W + K * W + 2 * PO * R * W), transcendentals=0
        ),
    )(
        segment_adapter, adapter_slot, live_segments,
        layer_input.reshape(T, L, W), output_grad, key_weight, adapter_down, adapter_up,
    )
    results = (input_grad, down_grad, up_grad)
    input_grad, down_grad, up_grad = pl.pallas_call(
        store_kernel,
        out_shape=tuple(jax.ShapeDtypeStruct(r.shape, r.dtype) for r in results),
        in_specs=[hbm] * 3,
        out_specs=(hbm,) * 3,
        scratch_shapes=[V(r.shape, r.dtype) for r in results] + [DMA((7,)), DMA((7,))],
        compiler_params=pltpu.CompilerParams(vmem_limit_bytes=VMEM_LIMIT),
        cost_estimate=pl.CostEstimate(
            flops=0, bytes_accessed=4 * (T * L * W + PO * R * W), transcendentals=0
        ),
    )(*results)
    return input_grad.reshape(T * L, W), down_grad, up_grad


def on_device(
    layer_input,
    output_grad,
    key_weight,
    adapter_down,
    adapter_up,
    segment_adapter,
    adapter_slot,
    live_segments,
):
    tensor_size = lax.axis_size("tensor")
    position = lax.axis_index("tensor")
    group_count = lax.axis_size("dp")
    group_index = lax.axis_index("dp")
    row_count = output_grad.shape[0]
    tok_group = layer_input.shape[0]
    width_shard = layer_input.shape[1]
    key_width = output_grad.shape[1]
    key_shard = key_width // tensor_size
    adapters = adapter_slot.shape[0]
    rank_dim = adapter_down.shape[1]
    seg_total = segment_adapter.shape[0]
    seg_group = seg_total // group_count
    seg_len = tok_group // seg_group
    per_owner = adapters // group_count
    slot_ids = jnp.arange(adapters, dtype=jnp.int32)
    lookup = segment_adapter[:, None] == slot_ids[None, :]
    every_slot = jnp.sum(jnp.where(lookup, adapter_slot[None, :], 0), axis=1)
    seg_slot = lax.dynamic_slice_in_dim(every_slot, group_index * seg_group, seg_group)
    local_rows = position * row_count + jnp.arange(row_count, dtype=jnp.int32)
    live_rows = local_rows // seg_len < live_segments[0]
    masked = jnp.where(live_rows[:, None], output_grad, jnp.zeros_like(output_grad))
    whole = lax.all_gather(masked, "tensor", axis=0, tiled=True)
    stores = (
        lax.all_gather(adapter_down, "dp", axis=0, tiled=True),
        lax.all_gather(adapter_up, "dp", axis=0, tiled=True),
    )
    choose = (seg_slot[:, None] == slot_ids[None, :]).astype(jnp.bfloat16)
    down_seg = jnp.dot(choose, stores[0].reshape(adapters, -1), preferred_element_type=jnp.float32)
    down_seg = down_seg.astype(jnp.bfloat16).reshape(seg_group, rank_dim, width_shard)
    up_seg = jnp.dot(choose, stores[1].reshape(adapters, -1), preferred_element_type=jnp.float32)
    up_seg = up_seg.astype(jnp.bfloat16).reshape(seg_group, rank_dim, key_shard)
    own_keys = lax.dynamic_slice_in_dim(whole, position * key_shard, key_shard, 1).reshape(
        seg_group, seg_len, key_shard
    )
    input_seg = layer_input.reshape(seg_group, seg_len, width_shard)
    up_part = jnp.einsum("sjk,srk->rsj", own_keys, up_seg, preferred_element_type=jnp.float32)
    down_part = jnp.einsum("sjd,srd->rsj", input_seg, down_seg, preferred_element_type=jnp.float32)
    lowrank, projected = lax.psum((up_part, down_part), "tensor")
    lowrank = lowrank.astype(jnp.bfloat16)
    projected = projected.astype(jnp.bfloat16)
    frozen = lax.dot_general(
        whole, key_weight, (((1,), (1,)), ((), ())), preferred_element_type=jnp.float32
    )
    extra = jnp.einsum("rsj,srd->sjd", lowrank, down_seg, preferred_element_type=jnp.float32)
    input_grad = (frozen + 2.0 * extra.reshape(tok_group, width_shard)).astype(jnp.bfloat16)
    seg_down = 2.0 * jnp.einsum(
        "rsj,sjd->srd", lowrank, input_seg, preferred_element_type=jnp.float32
    )
    seg_up = 2.0 * jnp.einsum(
        "rsj,sjk->srk", projected, own_keys, preferred_element_type=jnp.float32
    )
    seg_index = jnp.arange(seg_group, dtype=jnp.int32)
    same = seg_slot[:, None] == seg_slot[None, :]
    earlier = same & (seg_index[None, :] < seg_index[:, None])
    leading = jnp.logical_not(jnp.any(earlier, axis=1))
    merge_rows = (same & leading[:, None]).astype(jnp.float32)
    rows_down = jnp.einsum(
        "us,srd->urd", merge_rows, seg_down, precision=lax.Precision.HIGHEST
    ).astype(jnp.bfloat16)
    rows_up = jnp.einsum("us,srk->urk", merge_rows, seg_up, precision=lax.Precision.HIGHEST).astype(
        jnp.bfloat16
    )
    every_down, every_up = (
        lax.all_gather(rows_down, "dp", axis=0, tiled=True),
        lax.all_gather(rows_up, "dp", axis=0, tiled=True),
    )
    owned = group_index * per_owner + jnp.arange(per_owner, dtype=jnp.int32)
    mine = (every_slot[:, None] == owned[None, :]).astype(jnp.bfloat16)
    down_grad = jnp.einsum(
        "sp,srd->prd", mine, every_down, preferred_element_type=jnp.float32
    ).astype(jnp.bfloat16)
    up_grad = jnp.einsum("sp,srk->prk", mine, every_up, preferred_element_type=jnp.float32).astype(
        jnp.bfloat16
    )
    return (input_grad, down_grad, up_grad)


def device_program(layer_input, output_grad, key_weight, adapter_down, adapter_up, segment_adapter, adapter_slot, live_segments):
    args = (layer_input, output_grad, key_weight, adapter_down, adapter_up, segment_adapter, adapter_slot, live_segments)
    seg_group = segment_adapter.shape[0] // lax.axis_size("dp")
    one_each = seg_group == lax.axis_size("tensor") == 8
    tiled = adapter_up.shape[2] % 128 == 0 and layer_input.shape[1] % 256 == 0
    if one_each and tiled and lax.axis_size("dp") % 2 == 0:
        return fused(*args)
    return on_device(*args)


def solution(mesh):
    in_specs = (
        P("dp", "tensor"),
        P(("dp", "tensor"), None),
        P("tensor", None),
        P("dp", None, "tensor"),
        P("dp", None, "tensor"),
        P(),
        P(),
        P("dp"),
    )
    out_specs = (P("dp", "tensor"), P("dp", None, "tensor"), P("dp", None, "tensor"))
    return jax.shard_map(
        device_program, mesh=mesh, in_specs=in_specs, out_specs=out_specs, check_vma=False
    )
```

```python
import functools

import jax
import jax.numpy as jnp
from jax import lax
from jax.experimental import pallas as pl
from jax.experimental.pallas import tpu as pltpu
from jax.sharding import PartitionSpec as P

MESH = pl.DeviceIdType.MESH
CHUNKS = 4
VMEM_LIMIT = 62 * 1024 * 1024
NT = (((1,), (1,)), ((), ()))
TN = (((0,), (0,)), ((), ()))


def fused_kernel(
    dims,
    adapter_hbm, slot_hbm, live_hbm,
    x_hbm, og_hbm, kw_hbm, ad_hbm, au_hbm,
    ig_hbm, dg_hbm, ug_hbm,
    adapter_s, slot_s, live_s, seg_slot, first,
    x_v, kw_v, ad_v, au_v, og_v, whole, ig_v, dg_v, ug_v,
    s1d_out, s1d_in, s2d_out, s2d_in, fu_out, fu_in,
    down_seg, up_seg, up_own, lr, pr_out, pr_in, su_out, su_in, rows_d, rows_u,
    load_sem, store_sem, blk_send, blk_recv, s1_send, s1_recv, s2_send, s2_recv, fu_send, fu_recv,
    up_send, up_recv, lr_send, lr_recv, pr_send, pr_recv, su_send, su_recv,
    rwy_send, rwu_send, rwc_send, rw_recv,
):
    T, X, Q, S, L, R, W, K, KS, PO = dims
    Z, Y = T // X, Q // 2
    half = L // CHUNKS
    t, q = lax.axis_index("tensor"), lax.axis_index("dp")
    z, x = t // X, lax.rem(t, X)
    y, c = q // 2, lax.rem(q, 2)
    mate = q + 1 - 2 * c
    pending = []

    def send(src, dst, send_sem, recv_sem, to, when=None):
        copy = pltpu.make_async_remote_copy(
            src_ref=src, dst_ref=dst, send_sem=send_sem, recv_sem=recv_sem,
            device_id=to, device_id_type=MESH,
        )
        if when is None:
            copy.start()
        else:
            pl.when(when)(copy.start)
        pending.append((when, copy))

    def arrived(ref, sem, when=None):
        copy = pltpu.make_async_copy(ref, ref, sem)
        if when is None:
            copy.wait()
        else:
            pl.when(when)(copy.wait)

    scalars = [
        pltpu.make_async_copy(adapter_hbm, adapter_s, load_sem.at[5]),
        pltpu.make_async_copy(slot_hbm, slot_s, load_sem.at[6]),
        pltpu.make_async_copy(live_hbm, live_s, load_sem.at[7]),
    ]
    loads = [
        pltpu.make_async_copy(og_hbm, og_v, load_sem.at[0]),
        pltpu.make_async_copy(au_hbm, au_v, load_sem.at[2]),
        pltpu.make_async_copy(ad_hbm, ad_v, load_sem.at[1]),
    ]
    later_loads = [
        pltpu.make_async_copy(x_hbm, x_v, load_sem.at[3]),
        pltpu.make_async_copy(kw_hbm, kw_v, load_sem.at[4]),
    ]
    tensor_peers = [lax.rem(t + j, T) for j in range(1, T)]
    far = [lax.rem(y + j, Y) for j in range(1, Y)]
    barrier = pltpu.get_barrier_semaphore()
    for peer in tensor_peers:
        pl.semaphore_signal(barrier, inc=1, device_id={"tensor": peer}, device_id_type=MESH)
    dp_peers = [lax.rem(q + j, Q) for j in range(1, Q)]
    for peer in dp_peers:
        pl.semaphore_signal(barrier, inc=1, device_id={"dp": peer}, device_id_type=MESH)

    for copy in scalars[2:] + loads[:1] + scalars[:2] + [loads[2], loads[1]]:
        copy.start()

    scalars[2].wait()
    loads[0].wait()
    live = t < live_s[0]
    own_rows = jnp.where(live, og_v[...], jnp.zeros((L, K), jnp.bfloat16))
    whole[t] = own_rows
    pl.semaphore_wait(barrier, T - 1 + Q - 1)

    def rows_of(origin, part):
        return whole.at[origin, pl.ds(part * half, half)]

    def to_z(origin, part, up, when):
        step = 1 if up else -1
        edge = (z + 1 < Z) if up else (z > 0)
        when = edge if when is None else jnp.logical_and(when, edge)
        ref = rows_of(origin, part)
        send(ref, ref, blk_send.at[origin, part, 0 if up else 1], blk_recv.at[origin, part],
             {"tensor": t + step * X}, when)

    def to_x(origin, part, when):
        ref = rows_of(origin, part)
        for j in range(1, X):
            to = z * X + lax.rem(x + j, X)
            send(ref, ref, blk_send.at[origin, part, 1 + j], blk_recv.at[origin, part],
                 {"tensor": to}, when)

    direct = CHUNKS // 2
    pair_z = z + 1 - 2 * lax.rem(z, 2)
    column = z * X + lax.rem(x + 1, X)
    def start_own(part):
        to_z(t, part, True, None)
        to_z(t, part, False, None)
        to_x(t, part, None)

    start_own(0)
    start_own(1)

    def forward(step, part):
        for sign in (-1, 1):
            row = z + sign * step
            inside = jnp.logical_and(row >= 0, row < Z)
            origin = jnp.where(inside, row, z) * X + x
            arrived(rows_of(origin, part), blk_recv.at[origin, part], inside)
            to_z(origin, part, sign < 0, inside)
            across = inside
            if part >= direct:
                across = jnp.logical_and(inside, row != pair_z)
            to_x(origin, part, across)

    def share(part):
        ref = rows_of(column, part)
        send(ref, ref, blk_send.at[column, part, 0], blk_recv.at[column, part],
             {"tensor": pair_z * X + x})

    def combine_down(i, carry):
        group, s = i // S, lax.rem(i, S)
        inside, local = owned((group * 2 + c) * S + s)
        s2d_out[group, s] = jnp.where(inside, ad_v[local], s1d_in[group, s])
        return carry

    for copy in scalars[:2]:
        copy.wait()
    for s in range(Q * S):
        seg_slot[s] = slot_s[adapter_s[s]]

    def owned(index):
        local = seg_slot[index] - q * PO
        inside = jnp.logical_and(local >= 0, local < PO)
        return inside, jnp.clip(local, 0, PO - 1)

    loads[2].wait()

    def choose_down(i, carry):
        group, s = i // S, lax.rem(i, S)
        inside, local = owned((group * 2 + 1 - c) * S + s)
        s1d_out[group, s] = jnp.where(inside, ad_v[local], jnp.zeros((R, W), jnp.bfloat16))
        return carry

    lax.fori_loop(0, Y * S, choose_down, 0)
    send(s1d_out, s1d_in, s1_send.at[0], s1_recv.at[0], {"dp": mate})

    loads[1].wait()

    def choose_up(i, carry):
        group, s = i // S, lax.rem(i, S)
        inside, local = owned(i)
        fu_out[group, s] = jnp.where(inside, au_v[local], jnp.zeros((R, KS), jnp.bfloat16))
        return carry

    lax.fori_loop(0, Q * S, choose_up, 0)
    for copy in later_loads:
        copy.start()
    for peer in dp_peers:
        send(fu_out.at[peer], fu_in.at[q], fu_send.at[peer], fu_recv.at[q], {"dp": peer})
    start_own(2)
    start_own(3)

    def first_of(p, carry):
        slot = q * PO + p
        for group in range(Q):
            index = jnp.int32(-1)
            for s in reversed(range(S)):
                index = jnp.where(seg_slot[group * S + s] == slot, jnp.int32(s), index)
            first[p * Q + group] = index
        return carry

    lax.fori_loop(0, PO, first_of, 0)

    arrived(s1d_in, s1_recv.at[0])
    part_segs = S // 2

    def segs(piece):
        return pl.ds(piece * part_segs, part_segs)

    for piece in range(2):
        def combine_piece(i, carry):
            return combine_down(i // part_segs * S + piece * part_segs + lax.rem(i, part_segs), carry)

        lax.fori_loop(0, Y * part_segs, combine_piece, 0)
        for other in far:
            send(s2d_out.at[other, segs(piece)], s2d_in.at[y, segs(piece)], s2_send.at[other, piece],
                 s2_recv.at[y, piece], {"dp": other * 2 + c})
    total = fu_out[q]
    for peer in dp_peers:
        arrived(fu_in.at[peer], fu_recv.at[peer])
        total = total + fu_in[peer]
    up_seg[...] = total
    for peer in tensor_peers:
        send(up_seg.at[peer], up_own.at[t], up_send.at[peer], up_recv.at[t], {"tensor": peer})
    up_own[t] = up_seg[t]

    forward(1, 0)

    for peer in tensor_peers:
        arrived(up_own.at[peer], up_recv.at[peer])
    acc = jnp.zeros((R, L), jnp.float32)
    for p in range(T):
        acc = acc + lax.dot_general(
            up_own[p], whole[t, :, p * KS:(p + 1) * KS], NT, preferred_element_type=jnp.float32
        )
    lr[t] = acc.astype(jnp.bfloat16)
    for peer in tensor_peers:
        send(lr.at[t], lr.at[t], lr_send.at[peer], lr_recv.at[t], {"tensor": peer})

    forward(1, 1)
    forward(1, 2)

    later_loads[0].wait()

    def down_of(s, carry):
        rows = s2d_out[y, s]
        for other in far:
            rows = rows + s2d_in[other, s]
        down_seg[s] = rows
        pr_out[s] = lax.dot_general(rows, x_v[s], NT, preferred_element_type=jnp.float32)
        return carry

    def project(piece):
        for other in far:
            arrived(s2d_in.at[other, segs(piece)], s2_recv.at[other, piece])
        lax.fori_loop(piece * part_segs, (piece + 1) * part_segs, down_of, 0, unroll=2)
        for s in range(piece * part_segs, (piece + 1) * part_segs):
            remote = s != t
            send(pr_out.at[s], pr_in.at[t], pr_send.at[s], pr_recv.at[t], {"tensor": s}, remote)

            @pl.when(s == t)
            def _():
                pr_in[t] = pr_out[s]

    project(0)
    forward(1, 3)

    for peer in tensor_peers:
        arrived(lr.at[peer], lr_recv.at[peer])

    own_slots = [seg_slot[q * S + s] for s in range(S)]

    def merged(parts, u, zero):
        return [jnp.where(own_slots[u] == own_slots[s], parts[s], zero) for s in range(S)]

    zero_l = jnp.zeros((R, L), jnp.bfloat16)
    ranks = [lr[s] for s in range(S)]
    left = jnp.concatenate(
        [jnp.concatenate(merged(ranks, u, zero_l), axis=1) for u in range(S)], axis=0
    )
    tile = 256
    for n in range(W // tile):
        columns = slice(n * tile, (n + 1) * tile)
        right = jnp.concatenate([x_v[s, :, columns] for s in range(S)], axis=0)
        grad = 2.0 * jnp.dot(left, right, preferred_element_type=jnp.float32)
        rows_d[q, :, :, columns] = grad.astype(jnp.bfloat16).reshape(S, R, tile)
    for other in far:
        send(rows_d.at[q], rows_d.at[q], rwy_send.at[other], rw_recv.at[q, 0],
             {"dp": other * 2 + c})
    send(rows_d.at[q], rows_d.at[q], rwc_send.at[q], rw_recv.at[q, 0], {"dp": mate})

    forward(2, 0)
    project(1)
    forward(2, 1)
    later_loads[1].wait()

    def two_blocks(pair):
        left_rows = jnp.concatenate([whole[origin] for origin in pair], axis=0)
        for n in range(W // tile):
            at = slice(n * tile, (n + 1) * tile)
            value = lax.dot_general(left_rows, kw_v[at, :], NT, preferred_element_type=jnp.float32)
            for j, origin in enumerate(pair):
                extra = lax.dot_general(
                    lr[origin], down_seg[origin, :, at], TN, preferred_element_type=jnp.float32
                )
                ig_v[origin, :, at] = (value[j * L:(j + 1) * L] + 2.0 * extra).astype(jnp.bfloat16)
        for origin in pair:
            pltpu.make_async_copy(ig_v.at[origin], ig_hbm.at[origin], store_sem.at[origin]).start()

    def wait_side(origin, parts):
        for part in parts:
            arrived(rows_of(origin, part), blk_recv.at[origin, part])

    lower = z < 2
    near_row, far_row = jnp.where(lower, 2, 1), jnp.where(lower, 3, 0)
    other = lax.rem(x + 1, X)

    wait_side(column, range(CHUNKS))
    two_blocks((t, column))
    forward(2, 2)

    for peer in tensor_peers:
        arrived(pr_in.at[peer], pr_recv.at[peer])
    acc = pr_in[0]
    for p in range(1, T):
        acc = acc + pr_in[p]
    projected = acc.astype(jnp.bfloat16)
    for p in range(T):
        su_out[p] = 2.0 * jnp.dot(
            projected, whole[t, :, p * KS:(p + 1) * KS], preferred_element_type=jnp.float32
        )
    for peer in tensor_peers:
        send(su_out.at[peer], su_in.at[t], su_send.at[peer], su_recv.at[t], {"tensor": peer})
    su_in[t] = su_out[t]

    forward(2, 3)
    for part in range(direct, CHUNKS):
        share(part)
    forward(3, 0)
    two_blocks((pair_z * X + x, near_row * X + x))
    forward(3, 1)

    for peer in tensor_peers:
        arrived(su_in.at[peer], su_recv.at[peer])
    zero_u = jnp.zeros((R, KS), jnp.float32)
    for u in range(S):
        total = zero_u
        for s in range(S):
            total = total + jnp.where(own_slots[u] == own_slots[s], su_in[s], zero_u)
        rows_u[q, u] = total.astype(jnp.bfloat16)
    for peer in dp_peers:
        send(rows_u.at[q], rows_u.at[q], rwu_send.at[peer], rw_recv.at[q, 1], {"dp": peer})

    settled = list(pending)
    pending.clear()
    forward(3, 2)
    for far_chip in far:
        origin = far_chip * 2 + c
        arrived(rows_d.at[origin], rw_recv.at[origin, 0])
        send(rows_d.at[origin], rows_d.at[origin], rwc_send.at[origin],
             rw_recv.at[origin, 0], {"dp": mate})
    forward(3, 3)
    wait_side(near_row * X + other, range(CHUNKS))
    two_blocks((far_row * X + x, near_row * X + other))

    for group in range(Y):
        origin = group * 2 + 1 - c
        arrived(rows_d.at[origin], rw_recv.at[origin, 0])

    def owner_sum(rows, out, p, width):
        total = jnp.zeros((R, width), jnp.float32)
        for group in range(Q):
            index = first[p * Q + group]
            row = rows[group, jnp.maximum(index, 0)].astype(jnp.float32)
            total += jnp.where(index >= 0, row, 0.0)
        out[p] = total.astype(jnp.bfloat16)

    def owner_down(p, carry):
        owner_sum(rows_d, dg_v, p, W)
        return carry

    def owner_up(p, carry):
        owner_sum(rows_u, ug_v, p, KS)
        return carry

    lax.fori_loop(0, PO, owner_down, 0, unroll=2)
    stores = [
        pltpu.make_async_copy(dg_v, dg_hbm, store_sem.at[T]),
        pltpu.make_async_copy(ug_v, ug_hbm, store_sem.at[T + 1]),
    ]
    stores[0].start()


    for peer in dp_peers:
        arrived(rows_u.at[peer], rw_recv.at[peer, 1])
    lax.fori_loop(0, PO, owner_up, 0, unroll=4)
    stores[1].start()

    def settle(sends):
        for when, copy in sends:
            if when is None:
                copy.wait_send()
            else:
                pl.when(when)(copy.wait_send)

    settle(settled)
    wait_side(far_row * X + other, range(CHUNKS))
    wait_side(pair_z * X + other, range(CHUNKS))
    two_blocks((pair_z * X + other, far_row * X + other))

    settle(pending)
    for origin in range(T):
        pltpu.make_async_copy(ig_v.at[origin], ig_hbm.at[origin], store_sem.at[origin]).wait()
    for copy in stores:
        copy.wait()


def store_kernel(a, b, c, a_out, b_out, c_out, a_v, b_v, c_v, in_sem, out_sem):
    moves = []
    for src, held, dst, pieces in ((a, a_v, a_out, 4), (b, b_v, b_out, 2), (c, c_v, c_out, 1)):
        count = src.shape[0] // pieces
        for i in range(pieces):
            at, n = pl.ds(i * count, count), len(moves)
            moves.append((
                pltpu.make_async_copy(src.at[at], held.at[at], in_sem.at[n]),
                pltpu.make_async_copy(held.at[at], dst.at[at], out_sem.at[n]),
            ))
    for load, _ in moves:
        load.start()
    for load, store in moves:
        load.wait()
        store.start()
    for _, store in moves:
        store.wait()


def fused(layer_input, output_grad, key_weight, adapter_down, adapter_up, segment_adapter, adapter_slot, live_segments):
    T, Q = lax.axis_size("tensor"), lax.axis_size("dp")
    X = 1 << ((T.bit_length() - 1) // 2)
    W = layer_input.shape[1]
    L, K = output_grad.shape
    PO, R, KS = adapter_up.shape
    S = segment_adapter.shape[0] // Q
    Y = Q // 2
    dims = (T, X, Q, S, L, R, W, K, KS, PO)
    bf, f32 = jnp.bfloat16, jnp.float32
    V, DMA = pltpu.VMEM, pltpu.SemaphoreType.DMA
    far_in = pl.BlockSpec(memory_space=pltpu.HBM)
    hbm = pl.BlockSpec(memory_space=pl.ANY)
    flops = 2 * T * L * K * W + 8 * T * L * R * W
    input_grad, down_grad, up_grad = pl.pallas_call(
        functools.partial(fused_kernel, dims),
        out_shape=(
            jax.ShapeDtypeStruct((T, L, W), bf),
            jax.ShapeDtypeStruct((PO, R, W), bf),
            jax.ShapeDtypeStruct((PO, R, KS), bf),
        ),
        in_specs=[far_in] * 8,
        out_specs=(hbm,) * 3,
        scratch_shapes=[
            pltpu.SMEM((Q * S,), jnp.int32), pltpu.SMEM((adapter_slot.shape[0],), jnp.int32),
            pltpu.SMEM((1,), jnp.int32), pltpu.SMEM((Q * S,), jnp.int32),
            pltpu.SMEM((PO * Q,), jnp.int32),
            V((T, L, W), bf), V((W, K), bf), V((PO, R, W), bf), V((PO, R, KS), bf), V((L, K), bf),
            V((T, L, K), bf), V((T, L, W), bf), V((PO, R, W), bf), V((PO, R, KS), bf),
            V((Y, S, R, W), bf), V((Y, S, R, W), bf), V((Y, S, R, W), bf), V((Y, S, R, W), bf),
            V((Q, S, R, KS), bf), V((Q, S, R, KS), bf),
            V((S, R, W), bf), V((S, R, KS), bf), V((T, R, KS), bf), V((T, R, L), bf),
            V((S, R, L), f32), V((T, R, L), f32), V((T, R, KS), f32), V((T, R, KS), f32),
            V((Q, S, R, W), bf), V((Q, S, R, KS), bf),
            DMA((8,)), DMA((T + 2,)), DMA((T, CHUNKS, 1 + X)), DMA((T, CHUNKS)),
            DMA((2,)), DMA((2,)), DMA((Y, 2)), DMA((Y, 2)), DMA((Q,)), DMA((Q,)),
            DMA((T,)), DMA((T,)), DMA((T,)), DMA((T,)),
            DMA((T,)), DMA((T,)), DMA((T,)), DMA((T,)),
            DMA((Y,)), DMA((Q,)), DMA((Q,)), DMA((Q, 2)),
        ],
        compiler_params=pltpu.CompilerParams(
            collective_id=0, has_side_effects=True, vmem_limit_bytes=VMEM_LIMIT
        ),
        cost_estimate=pl.CostEstimate(
            flops=flops, bytes_accessed=2 * (2 * T * L * W + K * W + 2 * PO * R * W), transcendentals=0
        ),
    )(
        segment_adapter, adapter_slot, live_segments,
        layer_input.reshape(T, L, W), output_grad, key_weight, adapter_down, adapter_up,
    )
    results = (input_grad, down_grad, up_grad)
    input_grad, down_grad, up_grad = pl.pallas_call(
        store_kernel,
        out_shape=tuple(jax.ShapeDtypeStruct(r.shape, r.dtype) for r in results),
        in_specs=[hbm] * 3,
        out_specs=(hbm,) * 3,
        scratch_shapes=[V(r.shape, r.dtype) for r in results] + [DMA((7,)), DMA((7,))],
        compiler_params=pltpu.CompilerParams(vmem_limit_bytes=VMEM_LIMIT),
        cost_estimate=pl.CostEstimate(
            flops=0, bytes_accessed=4 * (T * L * W + PO * R * W), transcendentals=0
        ),
    )(*results)
    return input_grad.reshape(T * L, W), down_grad, up_grad


def on_device(
    layer_input,
    output_grad,
    key_weight,
    adapter_down,
    adapter_up,
    segment_adapter,
    adapter_slot,
    live_segments,
):
    tensor_size = lax.axis_size("tensor")
    position = lax.axis_index("tensor")
    group_count = lax.axis_size("dp")
    group_index = lax.axis_index("dp")
    row_count = output_grad.shape[0]
    tok_group = layer_input.shape[0]
    width_shard = layer_input.shape[1]
    key_width = output_grad.shape[1]
    key_shard = key_width // tensor_size
    adapters = adapter_slot.shape[0]
    rank_dim = adapter_down.shape[1]
    seg_total = segment_adapter.shape[0]
    seg_group = seg_total // group_count
    seg_len = tok_group // seg_group
    per_owner = adapters // group_count
    slot_ids = jnp.arange(adapters, dtype=jnp.int32)
    lookup = segment_adapter[:, None] == slot_ids[None, :]
    every_slot = jnp.sum(jnp.where(lookup, adapter_slot[None, :], 0), axis=1)
    seg_slot = lax.dynamic_slice_in_dim(every_slot, group_index * seg_group, seg_group)
    local_rows = position * row_count + jnp.arange(row_count, dtype=jnp.int32)
    live_rows = local_rows // seg_len < live_segments[0]
    masked = jnp.where(live_rows[:, None], output_grad, jnp.zeros_like(output_grad))
    whole = lax.all_gather(masked, "tensor", axis=0, tiled=True)
    stores = (
        lax.all_gather(adapter_down, "dp", axis=0, tiled=True),
        lax.all_gather(adapter_up, "dp", axis=0, tiled=True),
    )
    choose = (seg_slot[:, None] == slot_ids[None, :]).astype(jnp.bfloat16)
    down_seg = jnp.dot(choose, stores[0].reshape(adapters, -1), preferred_element_type=jnp.float32)
    down_seg = down_seg.astype(jnp.bfloat16).reshape(seg_group, rank_dim, width_shard)
    up_seg = jnp.dot(choose, stores[1].reshape(adapters, -1), preferred_element_type=jnp.float32)
    up_seg = up_seg.astype(jnp.bfloat16).reshape(seg_group, rank_dim, key_shard)
    own_keys = lax.dynamic_slice_in_dim(whole, position * key_shard, key_shard, 1).reshape(
        seg_group, seg_len, key_shard
    )
    input_seg = layer_input.reshape(seg_group, seg_len, width_shard)
    up_part = jnp.einsum("sjk,srk->rsj", own_keys, up_seg, preferred_element_type=jnp.float32)
    down_part = jnp.einsum("sjd,srd->rsj", input_seg, down_seg, preferred_element_type=jnp.float32)
    lowrank, projected = lax.psum((up_part, down_part), "tensor")
    lowrank = lowrank.astype(jnp.bfloat16)
    projected = projected.astype(jnp.bfloat16)
    frozen = lax.dot_general(
        whole, key_weight, (((1,), (1,)), ((), ())), preferred_element_type=jnp.float32
    )
    extra = jnp.einsum("rsj,srd->sjd", lowrank, down_seg, preferred_element_type=jnp.float32)
    input_grad = (frozen + 2.0 * extra.reshape(tok_group, width_shard)).astype(jnp.bfloat16)
    seg_down = 2.0 * jnp.einsum(
        "rsj,sjd->srd", lowrank, input_seg, preferred_element_type=jnp.float32
    )
    seg_up = 2.0 * jnp.einsum(
        "rsj,sjk->srk", projected, own_keys, preferred_element_type=jnp.float32
    )
    seg_index = jnp.arange(seg_group, dtype=jnp.int32)
    same = seg_slot[:, None] == seg_slot[None, :]
    earlier = same & (seg_index[None, :] < seg_index[:, None])
    leading = jnp.logical_not(jnp.any(earlier, axis=1))
    merge_rows = (same & leading[:, None]).astype(jnp.float32)
    rows_down = jnp.einsum(
        "us,srd->urd", merge_rows, seg_down, precision=lax.Precision.HIGHEST
    ).astype(jnp.bfloat16)
    rows_up = jnp.einsum("us,srk->urk", merge_rows, seg_up, precision=lax.Precision.HIGHEST).astype(
        jnp.bfloat16
    )
    every_down, every_up = (
        lax.all_gather(rows_down, "dp", axis=0, tiled=True),
        lax.all_gather(rows_up, "dp", axis=0, tiled=True),
    )
    owned = group_index * per_owner + jnp.arange(per_owner, dtype=jnp.int32)
    mine = (every_slot[:, None] == owned[None, :]).astype(jnp.bfloat16)
    down_grad = jnp.einsum(
        "sp,srd->prd", mine, every_down, preferred_element_type=jnp.float32
    ).astype(jnp.bfloat16)
    up_grad = jnp.einsum("sp,srk->prk", mine, every_up, preferred_element_type=jnp.float32).astype(
        jnp.bfloat16
    )
    return (input_grad, down_grad, up_grad)


def device_program(layer_input, output_grad, key_weight, adapter_down, adapter_up, segment_adapter, adapter_slot, live_segments):
    args = (layer_input, output_grad, key_weight, adapter_down, adapter_up, segment_adapter, adapter_slot, live_segments)
    seg_group = segment_adapter.shape[0] // lax.axis_size("dp")
    one_each = seg_group == lax.axis_size("tensor") == 8
    tiled = adapter_up.shape[2] % 128 == 0 and layer_input.shape[1] % 256 == 0
    if one_each and tiled and lax.axis_size("dp") % 2 == 0:
        return fused(*args)
    return on_device(*args)


def solution(mesh):
    in_specs = (
        P("dp", "tensor"),
        P(("dp", "tensor"), None),
        P("tensor", None),
        P("dp", None, "tensor"),
        P("dp", None, "tensor"),
        P(),
        P(),
        P("dp"),
    )
    out_specs = (P("dp", "tensor"), P("dp", None, "tensor"), P("dp", None, "tensor"))
    return jax.shard_map(
        device_program, mesh=mesh, in_specs=in_specs, out_specs=out_specs, check_vma=False
    )
```
